32 devices in a mesh: section: 4 (over x, core), expert: 8 (over z, y).
Axes of the slice: x: 2, y: 2, z: 4, core: 2. Of those that a mesh axis runs over, the one named last changes fastest.
Arguments:
- act_in: bfloat16 [4, 1024, 6144], P('section', 'expert'), may hold values from -6 to 6
- saved_in: bfloat16 [4, 1024, 6144], P('section', 'expert'), may hold values from -6 to 6
- grad_in: bfloat16 [4, 1024, 6144], P('section', 'expert'), may hold values from -6 to 6
- fwd_routes: int32 [4, 1024, 2], P('section', 'expert'), may hold values from 0 to 7, as said below
- bwd_routes: int32 [4, 1024, 2], P('section', 'expert'), may hold values from 0 to 7, as said below
- w_gate: bfloat16 [4, 6144, 8192], P('section', None, 'expert'), may hold values from -0.078125 to 0.078125
- w_up: bfloat16 [4, 6144, 8192], P('section', None, 'expert'), may hold values from -0.078125 to 0.078125
- w_down: bfloat16 [4, 8192, 6144], P('section', 'expert'), may hold values from -0.0625 to 0.0625
- router: float32 [4, 6144, 8], P('section'), may hold values from -0.078125 to 0.078125
- norm_gain: float32 [4, 6144], P('section'), may hold values from 0.1 to 1.9
Outputs:
- act_out: bfloat16 [4, 1024, 6144], P('section', 'expert')
- grad_out: bfloat16 [4, 1024, 6144], P('section', 'expert')
The draws below stay inside these ranges and needn't reach their ends.
Inputs may be any that keep to these rules, and one draw needn't show every extreme that they name: `fwd_routes`: per section, the 128 rows of one device name expert 0 between 16 and 32 times, and in every section some device's rows name it exactly 32 times; a token's two experts differ. `bwd_routes`: per section, the 128 rows of one device name expert 0 between 16 and 32 times, and in every section some device's rows name it exactly 32 times; a token's two experts differ.
All inputs are finite; a program needn't handle non-finite values.
Results may differ from the reference program's by a relative error of at most 0.007.
Values may be sent and summed in bfloat16 or wider, within the bound.
No kernel may reach another device: no remote copies, remote signals or barrier semaphores. Data moves between devices by JAX's collectives and lax.ppermute only.
A program may use at most 128 MiB of HBM per device.

```python
import jax
import jax.numpy as jnp
from jax import lax

D = 6144
EXPERTS = 8
HID = 8192
TOK_DEV = 128
SECTIONS = 4
TOKENS = 1024
CAP = 32
N_EXPERT = 8


def window_routes(key):
    keys = jax.random.split(key, 6)
    blocks = SECTIONS * N_EXPERT
    counts = jax.random.randint(keys[0], (blocks,), CAP // 2, CAP + 1)
    forced = jax.random.randint(keys[1], (SECTIONS,), 0, N_EXPERT)
    block_ids = jnp.arange(blocks, dtype=jnp.int32)
    counts = jnp.where(block_ids % N_EXPERT == forced[block_ids // N_EXPERT], CAP, counts)
    shuffled = jax.vmap(lambda subkey: jax.random.permutation(subkey, TOK_DEV))(jax.random.split(keys[2], blocks))
    rank_in = jnp.argsort(shuffled, axis=1, stable=True)
    has_zero = rank_in < counts[:, None]
    first_pick = jax.random.randint(keys[3], (blocks, TOK_DEV), 1, EXPERTS)
    second_pick = jax.random.randint(keys[4], (blocks, TOK_DEV), 1, EXPERTS - 1)
    second_pick = second_pick + (second_pick >= first_pick).astype(jnp.int32)
    which_side = jax.random.randint(keys[5], (blocks, TOK_DEV), 0, 2)
    one_id = jnp.where(has_zero, jnp.where(which_side == 0, 0, first_pick), first_pick)
    two_id = jnp.where(has_zero, jnp.where(which_side == 0, first_pick, 0), second_pick)
    return jnp.stack([one_id, two_id], axis=2).reshape(SECTIONS, TOKENS, 2).astype(jnp.int32)


def draw_fwd_routes(key, part):
    return window_routes(jax.random.fold_in(key, 11))


def draw_bwd_routes(key, part):
    return window_routes(jax.random.fold_in(key, 23))


def shard_levels(own_key, shape, cuts, low, largest):
    def one(axis_at, parts):
        steps = jax.random.uniform(jax.random.fold_in(jax.random.fold_in(own_key, 6), axis_at), (parts,), jnp.float32, low / len(cuts), largest / len(cuts))
        return jnp.repeat(jnp.exp(steps), shape[axis_at] // parts).reshape((-1,) + (1,) * (len(shape) - axis_at - 1))

    loudness = one(*cuts[0])
    for cut in cuts[1:]:
        loudness = loudness * one(*cut)
    return loudness


def noise(own_key, extent, spread, limit, pieces=(), kind=jnp.bfloat16):
    loudness = shard_levels(own_key, extent, pieces, -0.22, 0.18) if pieces else 1.0
    entries = jax.random.normal(own_key, extent, jnp.float32) * spread * loudness
    return jnp.minimum(jnp.maximum(entries, -limit), limit).astype(kind)


def setup_inputs(seed: int = 0) -> dict:
    arg_keys = jax.random.split(jax.random.key(seed), 11)
    act_in = noise(arg_keys[0], (SECTIONS, TOKENS, D), 1.0, 6.0, ((0, 4), (1, 8)))
    saved_in = noise(arg_keys[1], (SECTIONS, TOKENS, D), 1.0, 6.0, ((0, 4), (1, 8)))
    grad_in = noise(arg_keys[2], (SECTIONS, TOKENS, D), 1.0, 6.0, ((0, 4), (1, 8)))
    fwd_routes = draw_fwd_routes(jax.random.fold_in(arg_keys[10], 71), 0)
    bwd_routes = draw_bwd_routes(jax.random.fold_in(arg_keys[10], 71), 0)
    w_gate = noise(arg_keys[5], (SECTIONS, D, HID), D ** -0.5, 0.078125, ((0, 4), (2, 8)))
    w_up = noise(arg_keys[6], (SECTIONS, D, HID), D ** -0.5, 0.078125, ((0, 4), (2, 8)))
    w_down = noise(arg_keys[7], (SECTIONS, HID, D), HID ** -0.5, 0.0625, ((0, 4), (1, 8)))
    router = noise(arg_keys[8], (SECTIONS, D, EXPERTS), D ** -0.5, 0.078125, ((0, 4),), jnp.float32)
    norm_gain = jnp.clip(1.0 + 0.18 * jax.random.normal(arg_keys[9], (SECTIONS, D), jnp.float32), 0.1, 1.9)
    return {"act_in": act_in, "saved_in": saved_in, "grad_in": grad_in, "fwd_routes": fwd_routes, "bwd_routes": bwd_routes, "w_gate": w_gate, "w_up": w_up, "w_down": w_down, "router": router, "norm_gain": norm_gain}


epsilon = 1e-05
highest = lax.Precision.HIGHEST

def norm_route(inputs, gain_row, router_mat, chosen_ids):
    inverse = lax.rsqrt(lax.optimization_barrier(jnp.mean(inputs * inputs, axis=1, keepdims=True)) + epsilon)
    normed = inputs * inverse * gain_row[None, :]
    logits = jnp.dot(normed, router_mat, precision=highest)
    onehot = (chosen_ids[:, :, None] == jnp.arange(router_mat.shape[1], dtype=jnp.int32)[None, None, :]).astype(jnp.float32)
    picked = lax.optimization_barrier(jnp.sum(onehot * logits[:, None, :], axis=2))
    first_share = jax.nn.sigmoid(picked[:, 0] - picked[:, 1])
    shares = jnp.stack([first_share, 1.0 - first_share], axis=1)
    window_weight = lax.optimization_barrier(jnp.sum(shares * (chosen_ids == 0).astype(jnp.float32), axis=1))
    return (normed, window_weight)

def assign_window(chosen_ids, capacity):
    named_zero = lax.optimization_barrier(jnp.sum((chosen_ids == 0).astype(jnp.int32), axis=1))
    rank_in = jnp.cumsum(named_zero) - named_zero
    slot_of = jnp.where(named_zero > 0, rank_in, capacity).astype(jnp.int32)
    matches = (slot_of[None, :] == jnp.arange(capacity, dtype=jnp.int32)[:, None]).astype(jnp.int32)
    token_ids = jnp.arange(chosen_ids.shape[0], dtype=jnp.int32) + 1
    source = (lax.optimization_barrier(jnp.sum(matches * token_ids[None, :], axis=1)) - 1).astype(jnp.int32)
    return (slot_of, source)

def fill_rows(values, source):
    picked = jnp.take(values, jnp.maximum(source, 0), axis=0)
    keep = (source >= 0).reshape((-1,) + (1,) * (values.ndim - 1))
    return jnp.where(keep, picked, jnp.zeros_like(picked))

def unfill(lookup, slot_of):
    padded = jnp.concatenate([lookup, jnp.zeros((1,) + lookup.shape[1:], lookup.dtype)], axis=0)
    return jnp.take(padded, slot_of, axis=0)

def forward_part(slot_rows, gate_cols, up_cols, down_rows):
    gate_pre = jnp.dot(slot_rows, gate_cols, preferred_element_type=jnp.float32)
    up_pre = jnp.dot(slot_rows, up_cols, preferred_element_type=jnp.float32)
    active = (gate_pre * jax.nn.sigmoid(gate_pre) * up_pre).astype(jnp.bfloat16)
    return jnp.dot(active, down_rows, preferred_element_type=jnp.float32).astype(jnp.bfloat16)

def backward_part(slot_rows, upstream_rows, weight_col, gate_cols, up_cols, down_rows):
    last_dims = (((1,), (1,)), ((), ()))
    gate_pre = jnp.dot(slot_rows, gate_cols, preferred_element_type=jnp.float32)
    up_pre = jnp.dot(slot_rows, up_cols, preferred_element_type=jnp.float32)
    gate_sig = jax.nn.sigmoid(gate_pre)
    silu_val = gate_pre * gate_sig
    active = (silu_val * up_pre).astype(jnp.bfloat16)
    back_cols = lax.dot_general(upstream_rows, down_rows, last_dims, preferred_element_type=jnp.float32)
    slope_part = lax.optimization_barrier(jnp.sum(active.astype(jnp.float32) * back_cols, axis=1)).astype(jnp.bfloat16)
    act_cot = weight_col[:, None] * back_cols
    gate_cot = (act_cot * up_pre * gate_sig * (1.0 + gate_pre * (1.0 - gate_sig))).astype(jnp.bfloat16)
    up_cot = (act_cot * silu_val).astype(jnp.bfloat16)
    row_part = (lax.dot_general(gate_cot, gate_cols, last_dims, preferred_element_type=jnp.float32) + lax.dot_general(up_cot, up_cols, last_dims, preferred_element_type=jnp.float32)).astype(jnp.bfloat16)
    return (row_part, slope_part)

def reference(act_in, saved_in, grad_in, fwd_routes, bwd_routes, w_gate, w_up, w_down, router, norm_gain):
    hid_dev = HID // N_EXPERT
    slot_total = N_EXPERT * CAP

    def assign(chosen_ids):
        return assign_window(chosen_ids, CAP)

    def one_section(section_pos):
        gate_all = lax.dynamic_index_in_dim(w_gate, section_pos, 0, keepdims=False)
        up_all = lax.dynamic_index_in_dim(w_up, section_pos, 0, keepdims=False)
        down_all = lax.dynamic_index_in_dim(w_down, section_pos, 0, keepdims=False)
        router_mat = lax.dynamic_index_in_dim(router, section_pos, 0, keepdims=False)
        gain_row = lax.dynamic_index_in_dim(norm_gain, section_pos, 0, keepdims=False)
        fwd_x = lax.dynamic_index_in_dim(act_in, section_pos, 0, keepdims=False).astype(jnp.float32)
        fwd_ids = lax.dynamic_index_in_dim(fwd_routes, section_pos, 0, keepdims=False)
        normed_f, weight_f = norm_route(fwd_x, gain_row, router_mat, fwd_ids)
        slot_f, source_f = jax.vmap(assign)(fwd_ids.reshape(N_EXPERT, TOK_DEV, 2))
        rows_f = jax.vmap(fill_rows)(normed_f.astype(jnp.bfloat16).reshape(N_EXPERT, TOK_DEV, D), source_f)
        rows_f = rows_f.reshape(slot_total, D)
        back_x = lax.dynamic_index_in_dim(saved_in, section_pos, 0, keepdims=False).astype(jnp.float32)
        upstream = lax.dynamic_index_in_dim(grad_in, section_pos, 0, keepdims=False)
        bwd_ids = lax.dynamic_index_in_dim(bwd_routes, section_pos, 0, keepdims=False)

        def front(inputs):
            return norm_route(inputs, gain_row, router_mat, bwd_ids)
        (normed_b, weight_b), pullback = jax.vjp(front, back_x)
        slot_b, source_b = jax.vmap(assign)(bwd_ids.reshape(N_EXPERT, TOK_DEV, 2))
        rows_h = jax.vmap(fill_rows)(normed_b.astype(jnp.bfloat16).reshape(N_EXPERT, TOK_DEV, D), source_b)
        rows_u = jax.vmap(fill_rows)(upstream.reshape(N_EXPERT, TOK_DEV, D), source_b)
        rows_q = jax.vmap(fill_rows)(weight_b.astype(jnp.bfloat16).reshape(N_EXPERT, TOK_DEV), source_b)
        rows_h = rows_h.reshape(slot_total, D)
        rows_u = rows_u.reshape(slot_total, D)
        weight_col = rows_q.reshape(slot_total).astype(jnp.float32)

        def add_slice(slice_pos, running):
            first_col = (slice_pos * hid_dev).astype(jnp.int32)
            gate_cols = lax.dynamic_slice_in_dim(gate_all, first_col, hid_dev, 1)
            up_cols = lax.dynamic_slice_in_dim(up_all, first_col, hid_dev, 1)
            down_rows = lax.dynamic_slice_in_dim(down_all, first_col, hid_dev, 0)
            out_part = forward_part(rows_f, gate_cols, up_cols, down_rows)
            row_part, slope_part = backward_part(rows_h, rows_u, weight_col, gate_cols, up_cols, down_rows)
            return (running[0] + out_part.astype(jnp.float32), running[1] + row_part.astype(jnp.float32), running[2] + slope_part.astype(jnp.float32))
        initial = (jnp.zeros((slot_total, D), jnp.float32), jnp.zeros((slot_total, D), jnp.float32), jnp.zeros((slot_total,), jnp.float32))
        expert_out, row_cot, slope_sum = lax.fori_loop(0, N_EXPERT, add_slice, initial)
        picked_f = jax.vmap(unfill)(expert_out.reshape(N_EXPERT, CAP, D), slot_f).reshape(TOKENS, D)
        layer_out = (fwd_x + weight_f[:, None] * picked_f).astype(jnp.bfloat16)
        cot_normed = jax.vmap(unfill)(row_cot.reshape(N_EXPERT, CAP, D), slot_b).reshape(TOKENS, D)
        cot_weight = jax.vmap(unfill)(slope_sum.reshape(N_EXPERT, CAP), slot_b).reshape(TOKENS)
        d_rows = pullback((cot_normed, cot_weight))[0]
        grad_rows = (upstream.astype(jnp.float32) + d_rows).astype(jnp.bfloat16)
        return (layer_out, grad_rows)
    results = lax.map(one_section, jnp.arange(SECTIONS, dtype=jnp.int32))
    act_out = jnp.roll(results[0], 1, axis=0)
    grad_out = jnp.roll(results[1], -1, axis=0)
    return (act_out, grad_out)
```

```python
import jax
import jax.numpy as jnp
from jax import lax
from jax.experimental import pallas as pl
from jax.experimental.pallas import tpu as pltpu
from jax.sharding import PartitionSpec as P

epsilon = 1e-05
highest = lax.Precision.HIGHEST
f32 = jnp.float32
bf16 = jnp.bfloat16
last_dims = (((1,), (1,)), ((), ()))
vmem_limit = 48 * 1024 * 1024


def ring_of(count):
    return list(range(0, count, 2)) + list(range(1, count, 2))[::-1]


def hop(value, steps):
    ring = ring_of(lax.axis_size("expert"))
    count = len(ring)
    return lax.ppermute(value, "expert", [(ring[i], ring[(i + steps) % count]) for i in range(count)])


def shifted(value, steps):
    count = lax.axis_size("section")
    return lax.ppermute(value, "section", [(source, (source + steps) % count) for source in range(count)])


def halves(value):
    middle = value.shape[1] // 2
    return [value[:, :middle], value[:, middle:]]


def reach(count, chunk):
    far, near = count // 2, (count - 1) // 2
    return (far, near) if chunk == 0 else (near, far)


def ring_gather(chunks):
    count = lax.axis_size("expert")
    held = [[None] * count for _ in chunks]
    state = []
    for c, value in enumerate(chunks):
        held[c][0] = value
        state.append([value, value])
    for step in range(count // 2):
        for c in range(len(chunks)):
            for way in (0, 1):
                if step < reach(count, c)[way]:
                    state[c][way] = hop(state[c][way], 1 - 2 * way)
                    held[c][(-1 - step) % count if way == 0 else step + 1] = state[c][way]
    return held


def ring_scatter(parts):
    count = lax.axis_size("expert")
    state = []
    for c in range(len(parts)):
        fore, back = reach(count, c)
        state.append([parts[c][fore], parts[c][-back % count]])
    for step in range(count // 2):
        for c in range(len(parts)):
            for way in (0, 1):
                left = reach(count, c)[way] - step
                if left <= 0:
                    continue
                value = hop(state[c][way], 1 - 2 * way)
                if left > 1:
                    own = parts[c][(left - 1) if way == 0 else (1 - left) % count]
                    value = (value.astype(f32) + own.astype(f32)).astype(bf16)
                state[c][way] = value
    return [
        parts[c][0].astype(f32) + state[c][0].astype(f32) + state[c][1].astype(f32) for c in range(len(parts))
    ]


def cost(flops, moved):
    return pl.CostEstimate(flops=int(flops), bytes_accessed=int(moved), transcendentals=0)


def params():
    return pltpu.CompilerParams(vmem_limit_bytes=vmem_limit)


def dot_t(left, right):
    return lax.dot_general(left, right, last_dims, preferred_element_type=f32)


def dot_n(left, right):
    return jnp.dot(left, right, preferred_element_type=f32)


def whole(array):
    return pl.BlockSpec(array.shape, lambda i: (0,) * array.ndim)


def back_kernel(rows_ref, down_ref, out_ref):
    out_ref[...] = dot_t(rows_ref[...], down_ref[...])


def back_call(rows, down):
    count, width = rows.shape
    hid = down.shape[0]
    block = min(256, hid)
    return pl.pallas_call(
        back_kernel,
        grid=(hid // block,),
        in_specs=[whole(rows), pl.BlockSpec((block, width), lambda i: (i, 0))],
        out_specs=pl.BlockSpec((count, block), lambda i: (0, i)),
        out_shape=jax.ShapeDtypeStruct((count, hid), f32),
        compiler_params=params(),
        cost_estimate=cost(2 * count * width * hid, 2 * width * (hid + count)),
    )(rows, down)


def cots_kernel(rows_ref, gate_ref, up_ref, back_ref, gate_cot_ref, up_cot_ref, slope_ref):
    gate_pre = dot_n(rows_ref[...], gate_ref[...])
    up_pre = dot_n(rows_ref[...], up_ref[...])
    sig = jax.nn.sigmoid(gate_pre)
    silu = gate_pre * sig
    back = back_ref[...]
    active = (silu * up_pre).astype(bf16).astype(f32)
    part = jnp.sum(active * back, axis=1, keepdims=True)

    @pl.when(pl.program_id(0) == 0)
    def _():
        slope_ref[...] = jnp.zeros_like(slope_ref)

    slope_ref[...] += jnp.broadcast_to(part, slope_ref.shape)
    gate_cot_ref[...] = (back * up_pre * sig * (1.0 + gate_pre * (1.0 - sig))).astype(bf16)
    up_cot_ref[...] = (back * silu).astype(bf16)


def cots_call(rows, gate, up, back):
    count, width = rows.shape
    hid = gate.shape[1]
    block = min(256, hid)
    wide = pl.BlockSpec((width, block), lambda i: (0, i))
    tall = pl.BlockSpec((count, block), lambda i: (0, i))
    return pl.pallas_call(
        cots_kernel,
        grid=(hid // block,),
        in_specs=[whole(rows), wide, wide, tall],
        out_specs=[tall, tall, pl.BlockSpec((count, 128), lambda i: (0, 0))],
        out_shape=[
            jax.ShapeDtypeStruct((count, hid), bf16),
            jax.ShapeDtypeStruct((count, hid), bf16),
            jax.ShapeDtypeStruct((count, 128), f32),
        ],
        compiler_params=params(),
        cost_estimate=cost(4 * count * width * hid, 2 * width * (2 * hid + count)),
    )(rows, gate, up, back)


def rowpart_kernel(gate_cot_ref, up_cot_ref, gate_ref, up_ref, out_ref):
    out_ref[...] = (
        dot_t(gate_cot_ref[...], gate_ref[...]) + dot_t(up_cot_ref[...], up_ref[...])
    ).astype(bf16)


def rowpart_call(gate_cot, up_cot, gate, up, chunk):
    count, hid = gate_cot.shape
    width = gate.shape[0] // 2
    block = 512 if width % 512 == 0 else 128
    steps = width // block
    wide = pl.BlockSpec((block, hid), lambda i: (i + chunk * steps, 0))
    return pl.pallas_call(
        rowpart_kernel,
        grid=(steps,),
        in_specs=[whole(gate_cot), whole(up_cot), wide, wide],
        out_specs=pl.BlockSpec((count, block), lambda i: (0, i)),
        out_shape=jax.ShapeDtypeStruct((count, width), bf16),
        compiler_params=params(),
        cost_estimate=cost(4 * count * width * hid, 4 * width * hid),
    )(gate_cot, up_cot, gate, up)


def active_kernel(rows_ref, gate_ref, up_ref, out_ref):
    gate_pre = dot_n(rows_ref[...], gate_ref[...])
    up_pre = dot_n(rows_ref[...], up_ref[...])
    out_ref[...] = (gate_pre * jax.nn.sigmoid(gate_pre) * up_pre).astype(bf16)


def active_call(rows, gate, up):
    count, width = rows.shape
    hid = gate.shape[1]
    block = min(256, hid)
    wide = pl.BlockSpec((width, block), lambda i: (0, i))
    return pl.pallas_call(
        active_kernel,
        grid=(hid // block,),
        in_specs=[whole(rows), wide, wide],
        out_specs=pl.BlockSpec((count, block), lambda i: (0, i)),
        out_shape=jax.ShapeDtypeStruct((count, hid), bf16),
        compiler_params=params(),
        cost_estimate=cost(4 * count * width * hid, 2 * width * (2 * hid + count)),
    )(rows, gate, up)


def outpart_kernel(active_ref, down_ref, out_ref):
    out_ref[...] = dot_n(active_ref[...], down_ref[...]).astype(bf16)


def outpart_call(active, down, chunk):
    count, hid = active.shape
    width = down.shape[1] // 2
    block = 512 if width % 512 == 0 else 128
    steps = width // block
    return pl.pallas_call(
        outpart_kernel,
        grid=(steps,),
        in_specs=[whole(active), pl.BlockSpec((hid, block), lambda i: (0, i + chunk * steps))],
        out_specs=pl.BlockSpec((count, block), lambda i: (0, i)),
        out_shape=jax.ShapeDtypeStruct((count, width), bf16),
        compiler_params=params(),
        cost_estimate=cost(2 * count * width * hid, 2 * width * hid),
    )(active, down)


def select_matrix(ids, capacity):
    tokens = ids.shape[0]
    named = jnp.sum((ids == 0).astype(bf16), axis=1)
    earlier = jnp.tril(jnp.ones((tokens, tokens), bf16), -1)
    rank = jnp.dot(earlier, named, preferred_element_type=f32)
    slot = jnp.where(named > 0, rank, float(capacity))
    return (slot[None, :] == jnp.arange(capacity, dtype=f32)[:, None]).astype(bf16)


def pick_ids(select, ids):
    return jnp.dot(select, ids.astype(bf16), preferred_element_type=f32).astype(jnp.int32)


def norm_route(inputs, gain_row, router_mat, chosen_ids):
    inverse = lax.rsqrt(jnp.mean(inputs * inputs, axis=1, keepdims=True) + epsilon)
    normed = inputs * inverse * gain_row[None, :]
    logits = jnp.dot(normed, router_mat, precision=highest)
    onehot = (
        chosen_ids[:, :, None] == jnp.arange(router_mat.shape[1], dtype=jnp.int32)[None, None, :]
    ).astype(f32)
    picked = jnp.sum(onehot * logits[:, None, :], axis=2)
    first_share = jax.nn.sigmoid(picked[:, 0] - picked[:, 1])
    shares = jnp.stack([first_share, 1.0 - first_share], axis=1)
    return (normed, jnp.sum(shares * (chosen_ids == 0).astype(f32), axis=1))


def split_rows(array, count):
    rows = array.shape[0] // count
    return [array[k * rows : (k + 1) * rows] for k in range(count)]


def joined(held):
    return jnp.concatenate([jnp.concatenate(shards, axis=0) for shards in held], axis=1)


def place(select, rows, base):
    spread = lax.dot_general(select, rows, (((0,), (0,)), ((), ())), preferred_element_type=f32).astype(bf16)
    used = jnp.sum(select.astype(f32), axis=0) > 0
    return jnp.where(used[:, None], spread, base)


def local(
    act_in, saved_in, grad_in, fwd_routes, bwd_routes, w_gate, w_up, w_down, router, norm_gain
):
    count = lax.axis_size("expert")
    capacity = act_in.shape[1] // 4
    gate, up, down = w_gate[0], w_up[0], w_down[0]
    gain_row, router_mat = norm_gain[0], router[0]
    fwd_ids, bwd_ids = fwd_routes[0], bwd_routes[0]

    select_b = select_matrix(bwd_ids, capacity)
    rows_u = jnp.dot(select_b, grad_in[0], preferred_element_type=f32)
    held_u = ring_gather(halves(rows_u.astype(bf16)))

    rows_b = jnp.dot(select_b, saved_in[0], preferred_element_type=f32)
    ids_b = pick_ids(select_b, bwd_ids)
    (normed_b, weight_b), pullback = jax.vjp(
        lambda inputs: norm_route(inputs, gain_row, router_mat, ids_b), rows_b
    )
    held_h = ring_gather(halves(normed_b.astype(bf16)))

    select_f = select_matrix(fwd_ids, capacity)
    rows_f = jnp.dot(select_f, act_in[0], preferred_element_type=f32)
    normed_f, weight_f = norm_route(rows_f, gain_row, router_mat, pick_ids(select_f, fwd_ids))
    held_f = ring_gather(halves(normed_f.astype(bf16)))

    act_base = shifted(act_in[0], 1)
    grad_base = shifted(grad_in[0], -1)
    select_f_there = shifted(select_f, 1)
    select_b_there = shifted(select_b, -1)

    back = back_call(joined(held_u), down)
    gate_cot, up_cot, slope = cots_call(joined(held_h), gate, up, back)
    row_parts = [split_rows(rowpart_call(gate_cot, up_cot, gate, up, c), count) for c in (0, 1)]
    slope_parts = split_rows(slope.astype(bf16), count)
    row_parts[1] = [jnp.concatenate(pair, axis=1) for pair in zip(row_parts[1], slope_parts, strict=True)]

    active = active_call(joined(held_f), gate, up)
    out_parts = [split_rows(outpart_call(active, down, c), count) for c in (0, 1)]

    sums = ring_scatter(row_parts)
    middle = sums[0].shape[1]
    scale = weight_b.astype(bf16).astype(f32)[:, None]
    cot_normed = jnp.concatenate([sums[0], sums[1][:, :middle]], axis=1) * scale
    d_rows = pullback((cot_normed, sums[1][:, middle]))[0]
    grad_rows = shifted((rows_u + d_rows).astype(bf16), -1)

    sums_f = ring_scatter(out_parts)
    layer_rows = [
        shifted((base + weight_f[:, None] * total).astype(bf16), 1)
        for base, total in zip(halves(rows_f), sums_f, strict=True)
    ]
    act_out = place(select_f_there, jnp.concatenate(layer_rows, axis=1), act_base)
    grad_out = place(select_b_there, grad_rows, grad_base)
    return (act_out[None], grad_out[None])


def solution(mesh):
    in_specs = (
        P("section", "expert", None),
        P("section", "expert", None),
        P("section", "expert", None),
        P("section", "expert", None),
        P("section", "expert", None),
        P("section", None, "expert"),
        P("section", None, "expert"),
        P("section", "expert", None),
        P("section", None, None),
        P("section", None),
    )
    out_specs = (P("section", "expert", None), P("section", "expert", None))
    return jax.shard_map(local, mesh=mesh, in_specs=in_specs, out_specs=out_specs, check_vma=False)
```

```python
import functools

import jax
import jax.numpy as jnp
from jax import lax
from jax.experimental import pallas as pl
from jax.experimental.pallas import tpu as pltpu
from jax.sharding import PartitionSpec as P

epsilon = 1e-05
highest = lax.Precision.HIGHEST
f32 = jnp.float32
bf16 = jnp.bfloat16
last_dims = (((1,), (1,)), ((), ()))


def ring_of(count):
    return list(range(0, count, 2)) + list(range(1, count, 2))[::-1]


def hop(value, steps):
    ring = ring_of(lax.axis_size("expert"))
    count = len(ring)
    return lax.ppermute(value, "expert", [(ring[i], ring[(i + steps) % count]) for i in range(count)])


def shifted(value, steps):
    count = lax.axis_size("section")
    return lax.ppermute(value, "section", [(source, (source + steps) % count) for source in range(count)])


def halves(value):
    middle = value.shape[1] // 2
    return [value[:, :middle], value[:, middle:]]


class Ring:

    def __init__(self):
        self.count = lax.axis_size("expert")
        self.full = (self.count - 1) // 2
        self.split = self.count % 2 == 0
        self.steps = self.full + self.split
        self.inbox = {}


class Gather(Ring):

    def begin(self, shard):
        self.held = [shard] + [None] * (self.count - 1)

    def send(self, step):
        ahead = self.held[-step % self.count]
        behind = self.held[step]
        if step == self.full:
            ahead, behind = halves(ahead)[0], halves(behind)[1]
        return [hop(ahead, 1), hop(behind, -1)]

    def receive(self, step, values):
        if step == self.full:
            self.held[step + 1] = jnp.concatenate(values, axis=1)
        else:
            self.held[-1 - step], self.held[step + 1] = values


class Scatter(Ring):

    def begin(self, part):
        self.parts = split_rows(part, self.count)

    def send(self, step):
        far = self.steps - step
        ahead, behind = self.parts[far], self.parts[-far]
        if self.split and step == 0:
            ahead, behind = halves(ahead)[0], halves(behind)[1]
        elif step > 0:
            ahead, behind = self.merged(ahead, 0, step), self.merged(behind, 1, step)
        return [hop(ahead, 1), hop(behind, -1)]

    def merged(self, own, way, step):
        value = self.inbox[way]
        if self.split and step == 1:
            pieces = halves(own)
            pieces[way] = (pieces[way].astype(f32) + value.astype(f32)).astype(bf16)
            return jnp.concatenate(pieces, axis=1)
        return (own.astype(f32) + value.astype(f32)).astype(bf16)

    def receive(self, step, values):
        self.inbox = dict(enumerate(values))

    def total(self):
        return sum(value.astype(f32) for value in (self.parts[0], *self.inbox.values()))


def fence(arrays):
    return pl.pallas_call(
        lambda *refs: None,
        in_specs=[pl.BlockSpec(memory_space=pl.ANY)] * len(arrays),
        out_specs=[pl.BlockSpec(memory_space=pl.ANY)] * len(arrays),
        out_shape=[jax.ShapeDtypeStruct(array.shape, array.dtype) for array in arrays],
        compiler_params=params(1),
        input_output_aliases={k: k for k in range(len(arrays))},
    )(*arrays)


class Shift:

    def __init__(self, array, steps, pieces):
        self.rows = split_rows(array, pieces)
        self.by = steps
        self.got = []

    def send(self, step):
        return [shifted(self.rows[step], self.by)]

    def receive(self, step, values):
        self.got += values

    def result(self):
        return jnp.concatenate(self.got, axis=0)


def run_windows(windows, pieces, env):
    flying, made = [], []
    for k, transfers in enumerate(windows):
        todo = pieces.get(k, [])
        names = list(made)
        for needs, _, _ in todo:
            names += [name for name in needs if name not in names]
        sources = [ring for ring, step in transfers if isinstance(ring, Gather) and step == 0]
        landed = [value for _, _, values in flying for value in values]
        passed = list(fence(landed + [env[name] for name in names] + [ring.held[0] for ring in sources]))
        for ring, step, values in flying:
            ring.receive(step, passed[: len(values)])
            passed = passed[len(values) :]
        for name in names:
            env[name] = passed.pop(0)
        for ring in sources:
            ring.held[0] = passed.pop(0)
        for ring, step in transfers:
            if isinstance(ring, Scatter) and step == 0:
                ring.begin(env[ring.source])
        with jax.named_scope(f"window_{k}"):
            flying = [(ring, step, ring.send(step)) for ring, step in transfers]
        made = []
        for needs, does, gives in todo:
            for name, value in zip(gives, does(*[env[name] for name in needs]), strict=True):
                env[name] = value
                made.append(name)
    for ring, step, values in flying:
        ring.receive(step, values)


def cost(flops, moved):
    return pl.CostEstimate(flops=int(flops), bytes_accessed=int(moved), transcendentals=0)


def params(mega):
    return pltpu.CompilerParams(vmem_limit_bytes=mega * 1024 * 1024)


def dot_t(left, right):
    return lax.dot_general(left, right, last_dims, preferred_element_type=f32)


def dot_n(left, right):
    return jnp.dot(left, right, preferred_element_type=f32)


in_hbm = pl.BlockSpec(memory_space=pltpu.HBM)
anywhere = pl.BlockSpec(memory_space=pl.ANY)
in_vmem = pl.BlockSpec(memory_space=pltpu.VMEM)


def pieces_of(length, most, grain):
    for number in range(most, 1, -1):
        if length % (number * grain) == 0:
            size = length // number
            return [slice(k * size, (k + 1) * size) for k in range(number)]
    return [slice(0, length)]


def row_copies(shards, rows_ref, sems):
    side = rows_ref.shape[0] // len(shards)
    return [
        pltpu.make_async_copy(shard, rows_ref.at[k * side : (k + 1) * side], sems.at[k])
        for k, shard in enumerate(shards)
    ]


def loads(source, target, parts, sems, columns=False):
    out = []
    for k, part in enumerate(parts):
        where = (slice(None), part) if columns else (part, slice(None))
        out.append(pltpu.make_async_copy(source.at[where], target.at[where], sems.at[k]))
    return out


def start_all(*lists):
    for group in zip(*lists, strict=True):
        for copy in group:
            copy.start()


def back_kernel(count, *refs):
    shards, (down_ref, out_ref, rows_ref, weight_ref, row_sems, sems) = refs[:count], refs[count:]
    parts = pieces_of(down_ref.shape[0], 4, 128)
    rows = row_copies(shards, rows_ref, row_sems)
    downs = loads(down_ref, weight_ref, parts, sems)
    start_all(rows)
    start_all(downs)
    for copy in rows:
        copy.wait()
    for part, copy in zip(parts, downs, strict=True):
        copy.wait()
        out_ref[:, part] = dot_t(rows_ref[...], weight_ref[part, :])


def back_call(shards, down):
    count, (side, width), hid = len(shards), shards[0].shape, down.shape[0]
    return pl.pallas_call(
        functools.partial(back_kernel, count),
        in_specs=[anywhere] * count + [in_hbm],
        out_specs=in_vmem,
        out_shape=jax.ShapeDtypeStruct((count * side, hid), f32),
        scratch_shapes=[
            pltpu.VMEM((count * side, width), bf16),
            pltpu.VMEM((hid, width), bf16),
            pltpu.SemaphoreType.DMA((count,)),
            pltpu.SemaphoreType.DMA((4,)),
        ],
        compiler_params=params(22),
        cost_estimate=cost(2 * count * side * width * hid, 2 * width * (hid + count * side)),
    )(*shards, down)


def gate_up(shards, gate_ref, up_ref, rows_ref, gate_w, up_w, gate_sum, up_sum, row_sems, gate_sems, up_sems):
    parts = pieces_of(gate_ref.shape[0], 6, 128)
    rows = row_copies(shards, rows_ref, row_sems)
    gates = loads(gate_ref, gate_w, parts, gate_sems)
    ups = loads(up_ref, up_w, parts, up_sems)
    start_all(rows)
    start_all(gates, ups)
    for copy in rows:
        copy.wait()
    for k, part in enumerate(parts):
        for copy, weight, total in ((gates[k], gate_w, gate_sum), (ups[k], up_w, up_sum)):
            copy.wait()
            product = dot_n(rows_ref[:, part], weight[part, :])
            total[...] = product if k == 0 else total[...] + product


def gate_up_scratch(count, side, width, hid):
    return [
        pltpu.VMEM((count * side, width), bf16),
        pltpu.VMEM((width, hid), bf16),
        pltpu.VMEM((width, hid), bf16),
        pltpu.VMEM((count * side, hid), f32),
        pltpu.VMEM((count * side, hid), f32),
        pltpu.SemaphoreType.DMA((count,)),
        pltpu.SemaphoreType.DMA((6,)),
        pltpu.SemaphoreType.DMA((6,)),
    ]


def cots_kernel(count, *refs):
    shards, (gate_ref, up_ref, back_ref, gate_cot_ref, up_cot_ref, slope_ref, *scratch) = refs[:count], refs[count:]
    gate_up(shards, gate_ref, up_ref, *scratch)
    gate_pre, up_pre = scratch[3][...], scratch[4][...]
    sig = jax.nn.sigmoid(gate_pre)
    silu = gate_pre * sig
    back = back_ref[...]
    active = (silu * up_pre).astype(bf16).astype(f32)
    slope_ref[...] = jnp.broadcast_to(
        jnp.sum(active * back, axis=1, keepdims=True), slope_ref.shape
    ).astype(slope_ref.dtype)
    gate_cot_ref[...] = (back * up_pre * sig * (1.0 + gate_pre * (1.0 - sig))).astype(bf16)
    up_cot_ref[...] = (back * silu).astype(bf16)


def cots_call(shards, gate, up, back):
    count, (side, width), hid = len(shards), shards[0].shape, gate.shape[1]
    return pl.pallas_call(
        functools.partial(cots_kernel, count),
        in_specs=[anywhere] * count + [in_hbm, in_hbm, in_vmem],
        out_specs=[in_vmem] * 3,
        out_shape=[
            jax.ShapeDtypeStruct((count * side, hid), bf16),
            jax.ShapeDtypeStruct((count * side, hid), bf16),
            jax.ShapeDtypeStruct((count * side, 128), bf16),
        ],
        scratch_shapes=gate_up_scratch(count, side, width, hid),
        compiler_params=params(44),
        cost_estimate=cost(4 * count * side * width * hid, 2 * width * (2 * hid + count * side)),
    )(*shards, gate, up, back)


def active_kernel(count, *refs):
    shards, (gate_ref, up_ref, out_ref, *scratch) = refs[:count], refs[count:]
    gate_up(shards, gate_ref, up_ref, *scratch)
    gate_pre = scratch[3][...]
    out_ref[...] = (gate_pre * jax.nn.sigmoid(gate_pre) * scratch[4][...]).astype(bf16)


def active_call(shards, gate, up):
    count, (side, width), hid = len(shards), shards[0].shape, gate.shape[1]
    return pl.pallas_call(
        functools.partial(active_kernel, count),
        in_specs=[anywhere] * count + [in_hbm, in_hbm],
        out_specs=in_vmem,
        out_shape=jax.ShapeDtypeStruct((count * side, hid), bf16),
        scratch_shapes=gate_up_scratch(count, side, width, hid),
        compiler_params=params(40),
        cost_estimate=cost(4 * count * side * width * hid, 2 * width * (2 * hid + count * side)),
    )(*shards, gate, up)


def rowpart_kernel(gate_cot_ref, up_cot_ref, slope_ref, gate_ref, up_ref, out_ref, gate_w, up_w, made, gate_sems, up_sems, out_sems):
    width = gate_ref.shape[0]
    parts = pieces_of(width, 6, 128)
    gates = loads(gate_ref, gate_w, parts, gate_sems)
    ups = loads(up_ref, up_w, parts, up_sems)
    start_all(gates, ups)
    made[:, width:] = slope_ref[...]
    outs = loads(made, out_ref, parts + [slice(width, made.shape[1])], out_sems, columns=True)
    outs[-1].start()
    for k, part in enumerate(parts):
        gates[k].wait()
        ups[k].wait()
        made[:, part] = (
            dot_t(gate_cot_ref[...], gate_w[part, :]) + dot_t(up_cot_ref[...], up_w[part, :])
        ).astype(bf16)
        outs[k].start()
    for copy in outs:
        copy.wait()


def rowpart_call(gate_cot, up_cot, slope, gate, up):
    count, hid = gate_cot.shape
    width, extra = gate.shape[0], slope.shape[1]
    return pl.pallas_call(
        rowpart_kernel,
        in_specs=[in_vmem] * 3 + [in_hbm] * 2,
        out_specs=anywhere,
        out_shape=jax.ShapeDtypeStruct((count, width + extra), bf16),
        scratch_shapes=[
            pltpu.VMEM((width, hid), bf16),
            pltpu.VMEM((width, hid), bf16),
            pltpu.VMEM((count, width + extra), bf16),
            pltpu.SemaphoreType.DMA((6,)),
            pltpu.SemaphoreType.DMA((6,)),
            pltpu.SemaphoreType.DMA((7,)),
        ],
        compiler_params=params(40),
        cost_estimate=cost(4 * count * width * hid, 4 * width * hid),
    )(gate_cot, up_cot, slope, gate, up)


def outpart_kernel(active_ref, down_ref, out_ref, down_w, made, sems, out_sems):
    parts = pieces_of(down_ref.shape[1], 6, 128)
    downs = loads(down_ref, down_w, parts, sems, columns=True)
    outs = loads(made, out_ref, parts, out_sems, columns=True)
    start_all(downs)
    for k, part in enumerate(parts):
        downs[k].wait()
        made[:, part] = dot_n(active_ref[...], down_w[:, part]).astype(bf16)
        outs[k].start()
    for copy in outs:
        copy.wait()


def outpart_call(active, down):
    count, hid = active.shape
    width = down.shape[1]
    return pl.pallas_call(
        outpart_kernel,
        in_specs=[in_vmem, in_hbm],
        out_specs=anywhere,
        out_shape=jax.ShapeDtypeStruct((count, width), bf16),
        scratch_shapes=[
            pltpu.VMEM((hid, width), bf16),
            pltpu.VMEM((count, width), bf16),
            pltpu.SemaphoreType.DMA((6,)),
            pltpu.SemaphoreType.DMA((6,)),
        ],
        compiler_params=params(22),
        cost_estimate=cost(2 * count * width * hid, 2 * width * hid),
    )(active, down)


def select_matrix(ids, capacity):
    tokens = ids.shape[0]
    named = jnp.sum((ids == 0).astype(bf16), axis=1)
    earlier = jnp.tril(jnp.ones((tokens, tokens), bf16), -1)
    rank = jnp.dot(earlier, named, preferred_element_type=f32)
    slot = jnp.where(named > 0, rank, float(capacity))
    return (slot[None, :] == jnp.arange(capacity, dtype=f32)[:, None]).astype(bf16)


def pick_ids(select, ids):
    return jnp.dot(select, ids.astype(bf16), preferred_element_type=f32).astype(jnp.int32)


def norm_route(inputs, gain_row, router_mat, chosen_ids):
    inverse = lax.rsqrt(jnp.mean(inputs * inputs, axis=1, keepdims=True) + epsilon)
    normed = inputs * inverse * gain_row[None, :]
    logits = jnp.dot(normed, router_mat, precision=highest)
    onehot = (
        chosen_ids[:, :, None] == jnp.arange(router_mat.shape[1], dtype=jnp.int32)[None, None, :]
    ).astype(f32)
    picked = jnp.sum(onehot * logits[:, None, :], axis=2)
    first_share = jax.nn.sigmoid(picked[:, 0] - picked[:, 1])
    shares = jnp.stack([first_share, 1.0 - first_share], axis=1)
    return (normed, jnp.sum(shares * (chosen_ids == 0).astype(f32), axis=1))


def split_rows(array, count):
    rows = array.shape[0] // count
    return [array[k * rows : (k + 1) * rows] for k in range(count)]


def place(select, rows, base):
    spread = lax.dot_general(select, rows, (((0,), (0,)), ((), ())), preferred_element_type=f32).astype(bf16)
    used = jnp.sum(select.astype(f32), axis=0) > 0
    return jnp.where(used[:, None], spread, base)


def local(
    act_in, saved_in, grad_in, fwd_routes, bwd_routes, w_gate, w_up, w_down, router, norm_gain
):
    count = lax.axis_size("expert")
    capacity = act_in.shape[1] // 4
    gate, up, down = w_gate[0], w_up[0], w_down[0]
    gain_row, router_mat = norm_gain[0], router[0]
    fwd_ids, bwd_ids = fwd_routes[0], bwd_routes[0]
    gather_u, gather_h, gather_f = Gather(), Gather(), Gather()
    scatter_r, scatter_o = Scatter(), Scatter()
    scatter_r.source, scatter_o.source = "row_part", "out_part"
    shift_act, shift_grad = Shift(act_in[0], 1, 4), Shift(grad_in[0], -1, 4)
    env = {}

    select_b = select_matrix(bwd_ids, capacity)
    env["select_b"], env["select_f"] = select_b, select_matrix(fwd_ids, capacity)
    rows_u = jnp.dot(select_b, grad_in[0], preferred_element_type=f32)
    gather_u.begin(rows_u.astype(bf16))

    def shifts(select_f, select_b):
        return (shifted(select_f, 1), shifted(select_b, -1))

    def front_b(select_b):
        rows_b = jnp.dot(select_b, saved_in[0], preferred_element_type=f32)
        ids_b = pick_ids(select_b, bwd_ids)
        (normed_b, weight_b), pullback = jax.vjp(
            lambda inputs: norm_route(inputs, gain_row, router_mat, ids_b), rows_b
        )
        env["pullback"] = pullback
        gather_h.begin(normed_b.astype(bf16))
        return (weight_b,)

    def front_f(select_f):
        rows_f = jnp.dot(select_f, act_in[0], preferred_element_type=f32)
        normed_f, weight_f = norm_route(rows_f, gain_row, router_mat, pick_ids(select_f, fwd_ids))
        gather_f.begin(normed_f.astype(bf16))
        return (rows_f, weight_f)

    def back():
        return (back_call(gather_u.held, down),)

    def active():
        return (active_call(gather_f.held, gate, up),)

    def outpart(active):
        return (outpart_call(active, down),)

    def cots(back):
        return cots_call(gather_h.held, gate, up, back)

    def rowpart(gate_cot, up_cot, slope):
        return (rowpart_call(gate_cot, up_cot, slope, gate, up),)

    windows = []
    for ring, merges in ((gather_u, False), (gather_f, True), (gather_h, True), (scatter_o, True), (scatter_r, True)):
        for step in range(ring.steps):
            if merges and step == 0:
                windows[-1].append((ring, step))
            else:
                windows.append([(ring, step)])
    start = {(ring, step): k for k, transfers in enumerate(windows) for ring, step in transfers}
    last = gather_u.steps - 1
    for k in range(4):
        windows[k] += [(shift_act, k), (shift_grad, k)]
    pieces = {}

    def put(window, needs, does, gives):
        pieces.setdefault(window, []).append((needs, does, gives))

    put(0, ("select_f",), front_f, ("rows_f", "weight_f"))
    put(1, ("select_b",), front_b, ("weight_b",))
    put(2, ("select_f", "select_b"), shifts, ("select_f_there", "select_b_there"))
    put(start[gather_u, last] + 1, (), back, ("back",))
    put(start[gather_f, last] + 1, (), active, ("active",))
    put(start[gather_h, last] - 1, ("active",), outpart, ("out_part",))
    put(start[gather_h, last] + 1, ("back",), cots, ("gate_cot", "up_cot", "slope"))
    put(start[scatter_o, last] - 1, ("gate_cot", "up_cot", "slope"), rowpart, ("row_part",))

    def act_rows(weight_f):
        return (shifted((env["rows_f"] + weight_f[:, None] * scatter_o.total()).astype(bf16), 1),)

    def act_place(select, rows):
        return (place(select, rows, shift_act.result()),)

    put(start[scatter_r, 0] + 1, ("weight_f",), act_rows, ("act_rows",))
    put(start[scatter_r, last], ("select_f_there", "act_rows"), act_place, ("act_out",))
    run_windows(windows, pieces, env)

    sums = scatter_r.total()
    width = gate.shape[0]
    scale = env["weight_b"].astype(bf16).astype(f32)[:, None]
    d_rows = env["pullback"]((sums[:, :width] * scale, sums[:, width]))[0]
    grad_rows = shifted((rows_u + d_rows).astype(bf16), -1)
    grad_out = place(env["select_b_there"], grad_rows, shift_grad.result())
    return (env["act_out"][None], grad_out[None])


def solution(mesh):
    in_specs = (
        P("section", "expert", None),
        P("section", "expert", None),
        P("section", "expert", None),
        P("section", "expert", None),
        P("section", "expert", None),
        P("section", None, "expert"),
        P("section", None, "expert"),
        P("section", "expert", None),
        P("section", None, None),
        P("section", None),
    )
    out_specs = (P("section", "expert", None), P("section", "expert", None))
    return jax.shard_map(local, mesh=mesh, in_specs=in_specs, out_specs=out_specs, check_vma=False)
```

```python
import functools

import jax
import jax.numpy as jnp
from jax import lax
from jax.experimental import pallas as pl
from jax.experimental.pallas import tpu as pltpu
from jax.sharding import PartitionSpec as P

epsilon = 1e-05
highest = lax.Precision.HIGHEST
f32 = jnp.float32
bf16 = jnp.bfloat16
last_dims = (((1,), (1,)), ((), ()))
first_dims = (((0,), (0,)), ((), ()))
in_hbm = pl.BlockSpec(memory_space=pltpu.HBM)
anywhere = pl.BlockSpec(memory_space=pl.ANY)
in_vmem = pl.BlockSpec(memory_space=pltpu.VMEM)


def shape_of(rows, columns, dtype=bf16):
    return jax.ShapeDtypeStruct((rows, columns), dtype)


def params(mega):
    return pltpu.CompilerParams(vmem_limit_bytes=mega * 1024 * 1024)


def cost(flops, moved):
    return pl.CostEstimate(flops=int(flops), bytes_accessed=int(moved), transcendentals=0)


def dot_t(left, right):
    return lax.dot_general(left, right, last_dims, preferred_element_type=f32)


def dot_n(left, right):
    return jnp.dot(left, right, preferred_element_type=f32)


def hop(value, steps):
    count = lax.axis_size("expert")
    ring = list(range(0, count, 2)) + list(range(1, count, 2))[::-1]
    return lax.ppermute(value, "expert", [(ring[i], ring[(i + steps) % count]) for i in range(count)])


def shifted(value, steps):
    count = lax.axis_size("section")
    return lax.ppermute(value, "section", [(source, (source + steps) % count) for source in range(count)])


def halves(value):
    middle = value.shape[1] // 2
    return [value[:, :middle], value[:, middle:]]


class Ring:

    def __init__(self, name):
        self.name = name
        self.count = lax.axis_size("expert")
        self.full = (self.count - 1) // 2
        self.split = self.count % 2 == 0
        self.steps = self.full + self.split


class Gather(Ring):

    def begin(self, shard):
        self.held = [[shard]] + [None] * (self.count - 1)

    def send(self, step):
        ahead = self.held[-step % self.count][0]
        behind = self.held[step][0]
        if step == self.full:
            ahead, behind = halves(ahead)[0], halves(behind)[1]
        return [hop(ahead, 1), hop(behind, -1)]

    def receive(self, step, values):
        if step == self.full:
            self.held[step + 1] = values
        else:
            self.held[-1 - step], self.held[step + 1] = [values[0]], [values[1]]

    def sources(self, step):
        return [self.held[0]] if step == 0 else []


class Scatter(Ring):

    def begin(self, parts):
        self.parts = parts

    def send(self, step):
        far = self.steps - step
        if step > 0:
            ahead, behind = merge_call(self.parts[far][0], self.inbox[0], self.parts[-far][0], self.inbox[1])
        else:
            ahead, behind = self.parts[far][0], self.parts[-far][-1]
        return [hop(ahead, 1), hop(behind, -1)]

    def receive(self, step, values):
        self.inbox = values

    def sources(self, step):
        return [self.parts[self.steps]] + [self.parts[-self.steps]] * (1 - self.split) if step == 0 else []


def fence(arrays):
    return list(
        pl.pallas_call(
            lambda *refs: None,
            in_specs=[anywhere] * len(arrays),
            out_specs=[anywhere] * len(arrays),
            out_shape=[jax.ShapeDtypeStruct(array.shape, array.dtype) for array in arrays],
            compiler_params=params(1),
            cost_estimate=cost(0, 0),
            input_output_aliases={k: k for k in range(len(arrays))},
        )(*arrays)
    )


def run_windows(windows, pieces, env):
    flying, made = [], []
    for k, transfers in enumerate(windows):
        todo = pieces.get(k, [])
        names = list(made)
        for needs, _, _ in todo:
            names += [name for name in needs if name not in names]
        sources = env.pop("renewed", [])
        for ring, step, _ in transfers:
            sources += [held for held in ring.sources(step) if not any(held is other for other in sources)]
        landing = [flight for flight in flying if flight[2] <= k]
        flying = [flight for flight in flying if flight[2] > k]
        landed = [value for _, _, _, values in landing for value in values]
        passed = fence(landed + [env[name] for name in names] + [value for held in sources for value in held])
        for ring, step, _, values in landing:
            ring.receive(step, passed[: len(values)])
            passed = passed[len(values) :]
        for name in names:
            env[name] = passed.pop(0)
        for held in sources:
            held[:] = [passed.pop(0) for _ in held]
        with jax.named_scope(f"window_{k}"):
            flying += [(ring, step, k + stay, ring.send(step)) for ring, step, stay in transfers]
        made = []
        for needs, does, gives in todo:
            for name, value in zip(gives, does(*[env[name] for name in needs]), strict=True):
                env[name] = value
                made.append(name)
    for ring, step, _, values in flying:
        ring.receive(step, values)


def pieces_of(length, most, grain):
    for number in range(most, 1, -1):
        if length % (number * grain) == 0:
            size = length // number
            return [slice(k * size, (k + 1) * size) for k in range(number)]
    return [slice(0, length)]


def flat(held):
    return [value for shard in held for value in shard]


def row_copies(held_shape, shards, rows_ref, sems):
    side = rows_ref.shape[0] // len(held_shape)
    copies, at = [], 0
    for k, widths in enumerate(held_shape):
        first = 0
        for wide in widths:
            target = rows_ref.at[k * side : (k + 1) * side, first : first + wide]
            copies.append(pltpu.make_async_copy(shards[at], target, sems.at[at]))
            first, at = first + wide, at + 1
    return copies


def widths_of(held):
    return tuple(tuple(value.shape[1] for value in shard) for shard in held)


def start_all(*lists):
    for group in zip(*lists, strict=True):
        for copy in group:
            copy.start()


def merge_kernel(own_a_ref, value_a_ref, own_b_ref, value_b_ref, out_a_ref, out_b_ref):
    for own_ref, value_ref, out_ref, first in (
        (own_a_ref, value_a_ref, out_a_ref, 0),
        (own_b_ref, value_b_ref, out_b_ref, own_b_ref.shape[1] - value_b_ref.shape[1]),
    ):
        here = slice(first, first + value_ref.shape[1])
        if value_ref.shape != own_ref.shape:
            out_ref[...] = own_ref[...]
        out_ref[:, here] = (own_ref[:, here].astype(f32) + value_ref[...].astype(f32)).astype(bf16)


def merge_call(own_a, value_a, own_b, value_b):
    return pl.pallas_call(
        merge_kernel,
        in_specs=[in_vmem] * 4,
        out_specs=[in_vmem] * 2,
        out_shape=[shape_of(*own.shape) for own in (own_a, own_b)],
        compiler_params=params(4),
        cost_estimate=cost(0, 6 * own_a.size),
    )(own_a, value_a, own_b, value_b)


def load_kernel(after_ref, source, target, flag_ref, sems):
    copies = [
        pltpu.make_async_copy(source.at[part], target.at[part], sems.at[k])
        for k, part in enumerate(pieces_of(source.shape[0], 4, 128))
    ]
    start_all(copies)
    flag_ref[...] = jnp.zeros_like(flag_ref)
    for copy in copies:
        copy.wait()


def load_call(after, weight):
    return pl.pallas_call(
        load_kernel,
        in_specs=[anywhere, in_hbm],
        out_specs=[in_vmem, in_vmem],
        out_shape=[pltpu.VMEM(weight.shape, weight.dtype), shape_of(8, 128, f32)],
        scratch_shapes=[pltpu.SemaphoreType.DMA((4,))],
        compiler_params=params(1),
        cost_estimate=cost(0, 4 * weight.size),
    )(after, weight)


def back_kernel(held_shape, *refs):
    count = sum(len(widths) for widths in held_shape)
    shards, (down_ref, out_ref, rows_ref, weight_ref, row_sems, sems) = refs[:count], refs[count:]
    parts = pieces_of(out_ref.shape[1], 4, 128)
    rows = row_copies(held_shape, shards, rows_ref, row_sems)
    downs = [
        pltpu.make_async_copy(down_ref.at[part], weight_ref.at[part], sems.at[k])
        for k, part in enumerate(parts)
    ]
    start_all(rows)
    start_all(downs)
    for copy in rows:
        copy.wait()
    for part, copy in zip(parts, downs, strict=True):
        copy.wait()
        out_ref[:, part] = dot_t(rows_ref[...], weight_ref[part, :])


def back_call(held, down):
    count, side, width, hid = len(held), held[0][0].shape[0], sum(widths_of(held)[0]), down.shape[0]
    return pl.pallas_call(
        functools.partial(back_kernel, widths_of(held)),
        in_specs=[anywhere] * len(flat(held)) + [in_hbm],
        out_specs=in_vmem,
        out_shape=shape_of(count * side, hid, f32),
        scratch_shapes=[
            pltpu.VMEM((count * side, width), bf16),
            pltpu.VMEM((hid, width), bf16),
            pltpu.SemaphoreType.DMA((len(flat(held)),)),
            pltpu.SemaphoreType.DMA((4,)),
        ],
        compiler_params=params(22),
        cost_estimate=cost(2 * count * side * width * hid, 2 * width * (hid + count * side)),
    )(*flat(held), down)


def gate_up(held_shape, shards, gate_ref, up_ref, rows_ref, gate_sum, up_sum, row_sems):
    rows = row_copies(held_shape, shards, rows_ref, row_sems)
    start_all(rows)
    for copy in rows:
        copy.wait()
    for k, part in enumerate(pieces_of(gate_ref.shape[0], 6, 128)):
        for weight, total in ((gate_ref, gate_sum), (up_ref, up_sum)):
            product = dot_n(rows_ref[:, part], weight[part, :])
            total[...] = product if k == 0 else total[...] + product


def gate_up_scratch(copies, count, side, width, hid):
    return [
        pltpu.VMEM((count * side, width), bf16),
        pltpu.VMEM((count * side, hid), f32),
        pltpu.VMEM((count * side, hid), f32),
        pltpu.SemaphoreType.DMA((copies,)),
    ]


def gate_up_cost(count, side, width, hid):
    return cost(4 * count * side * width * hid, 2 * width * (2 * hid + count * side))


def active_kernel(held_shape, *refs):
    count = sum(len(widths) for widths in held_shape)
    shards, (gate_ref, up_ref, out_ref, *scratch) = refs[:count], refs[count:]
    gate_up(held_shape, shards, gate_ref, up_ref, *scratch)
    gate_pre = scratch[1][...]
    out_ref[...] = (gate_pre * jax.nn.sigmoid(gate_pre) * scratch[2][...]).astype(bf16)


def active_call(held, gate, up):
    count, side, width, hid = len(held), held[0][0].shape[0], sum(widths_of(held)[0]), gate.shape[1]
    return pl.pallas_call(
        functools.partial(active_kernel, widths_of(held)),
        in_specs=[anywhere] * len(flat(held)) + [in_vmem] * 2,
        out_specs=in_vmem,
        out_shape=shape_of(count * side, hid),
        scratch_shapes=gate_up_scratch(len(flat(held)), count, side, width, hid),
        compiler_params=params(12),
        cost_estimate=gate_up_cost(count, side, width, hid),
    )(*flat(held), gate, up)


def cots_kernel(held_shape, *refs):
    count = sum(len(widths) for widths in held_shape)
    shards, (gate_ref, up_ref, back_ref, gate_cot_ref, up_cot_ref, slope_ref, *scratch) = refs[:count], refs[count:]
    gate_up(held_shape, shards, gate_ref, up_ref, *scratch)
    gate_pre, up_pre = scratch[1][...], scratch[2][...]
    sig = jax.nn.sigmoid(gate_pre)
    silu = gate_pre * sig
    back = back_ref[...]
    active = (silu * up_pre).astype(bf16).astype(f32)
    slope_ref[...] = jnp.broadcast_to(jnp.sum(active * back, axis=1, keepdims=True), slope_ref.shape)
    gate_cot_ref[...] = (back * up_pre * sig * (1.0 + gate_pre * (1.0 - sig))).astype(bf16)
    up_cot_ref[...] = (back * silu).astype(bf16)


def cots_call(held, gate, up, back):
    count, side, width, hid = len(held), held[0][0].shape[0], sum(widths_of(held)[0]), gate.shape[1]
    return pl.pallas_call(
        functools.partial(cots_kernel, widths_of(held)),
        in_specs=[anywhere] * len(flat(held)) + [in_vmem] * 3,
        out_specs=[in_vmem] * 3,
        out_shape=[
            shape_of(count * side, hid),
            shape_of(count * side, hid),
            shape_of(count * side, 128, f32),
        ],
        scratch_shapes=gate_up_scratch(len(flat(held)), count, side, width, hid),
        compiler_params=params(14),
        cost_estimate=gate_up_cost(count, side, width, hid),
    )(*flat(held), gate, up, back)


def segments(count, width, extra):
    whole, pair = [(0, width + extra)], [(0, width // 2), (width // 2, width + extra)]
    return [pair if 2 * k == count else whole for k in range(count)]


def part_shapes(side, held):
    return [shape_of(side, last - first) for ranges in held for first, last in ranges]


def spread(made, held, first, value):
    side, last, at = value.shape[0] // len(held), first + value.shape[1], 0
    for k, ranges in enumerate(held):
        for low, high in ranges:
            begin, end = max(first, low), min(last, high)
            if begin < end:
                rows = value[k * side : (k + 1) * side, begin - first : end - first]
                made[at][:, begin - low : end - low] = rows
            at += 1


def send_out(made, out_refs, sems):
    copies = [
        pltpu.make_async_copy(source, target, sems.at[at])
        for at, (source, target) in enumerate(zip(made, out_refs, strict=True))
    ]
    start_all(copies)
    for copy in copies:
        copy.wait()


def made_scratch(shapes):
    return [pltpu.VMEM(shape.shape, shape.dtype) for shape in shapes] + [pltpu.SemaphoreType.DMA((len(shapes),))]


def regroup(held, arrays):
    arrays = list(arrays)
    return [[arrays.pop(0) for _ in ranges] for ranges in held]


def outpart_kernel(held, active_ref, down_ref, *refs):
    number = sum(len(ranges) for ranges in held)
    out_refs, made, (out_sems, down_w, sems) = refs[:number], refs[number : 2 * number], refs[2 * number :]
    width = down_ref.shape[1]
    parts = pieces_of(width, 6, 128)
    downs = [
        pltpu.make_async_copy(down_ref.at[:, part], down_w.at[:, part], sems.at[k]) for k, part in enumerate(parts)
    ]
    start_all(downs)
    for part, copy in zip(parts, downs, strict=True):
        copy.wait()
        value = dot_n(active_ref[...], down_w[:, part])
        spread(made, held, part.start, value.astype(bf16))
    send_out(made, out_refs, out_sems)


def outpart_call(count, active, down):
    rows, (hid, width) = active.shape[0], down.shape
    held = segments(count, width, 0)
    shapes = part_shapes(rows // count, held)
    arrays = pl.pallas_call(
        functools.partial(outpart_kernel, held),
        in_specs=[in_vmem, in_hbm],
        out_specs=[anywhere] * len(shapes),
        out_shape=shapes,
        scratch_shapes=made_scratch(shapes) + [pltpu.VMEM((hid, width), bf16), pltpu.SemaphoreType.DMA((6,))],
        compiler_params=params(22),
        cost_estimate=cost(2 * rows * width * hid, 2 * width * hid),
    )(active, down)
    return regroup(held, arrays)


def rowpart_kernel(held, gate_cot_ref, up_cot_ref, slope_ref, gate_ref, up_ref, *refs):
    out_refs, (up_w, up_sems) = refs[:-2], refs[-2:]
    width = gate_ref.shape[0]
    parts = pieces_of(width, 6, 128)

    ups = [pltpu.make_async_copy(up_ref.at[part], up_w.at[part], up_sems.at[k]) for k, part in enumerate(parts)]
    start_all(ups)
    spread(out_refs, held, width, slope_ref[...].astype(bf16))
    for part, copy in zip(parts, ups, strict=True):
        value = dot_t(gate_cot_ref[...], gate_ref[part, :])
        copy.wait()
        value = value + dot_t(up_cot_ref[...], up_w[part, :])
        spread(out_refs, held, part.start, value.astype(bf16))


def rowpart_call(count, gate_cot, up_cot, slope, gate, up):
    rows, (width, hid) = gate_cot.shape[0], gate.shape
    held = segments(count, width, slope.shape[1])
    shapes = part_shapes(rows // count, held)
    arrays = pl.pallas_call(
        functools.partial(rowpart_kernel, held),
        in_specs=[in_vmem] * 4 + [in_hbm],
        out_specs=[in_vmem] * len(shapes),
        out_shape=shapes,
        scratch_shapes=[pltpu.VMEM((width, hid), bf16), pltpu.SemaphoreType.DMA((6,))],
        compiler_params=params(20),
        cost_estimate=cost(4 * rows * width * hid, 4 * width * hid),
    )(gate_cot, up_cot, slope, gate, up)
    return regroup(held, arrays)


def select_of(ids):
    tokens = ids.shape[1]
    capacity = tokens // 4
    named = jnp.max((ids == 0).astype(f32), axis=0, keepdims=True)
    row = lax.broadcasted_iota(jnp.int32, (tokens, tokens), 0)
    column = lax.broadcasted_iota(jnp.int32, (tokens, tokens), 1)
    earlier = (row < column).astype(bf16)
    rank = dot_n(jnp.broadcast_to(named, (8, tokens)).astype(bf16), earlier)[:1]
    slot = jnp.where(named > 0, rank, float(capacity))
    places = lax.broadcasted_iota(jnp.int32, (capacity, tokens), 0).astype(f32)
    return (slot == places).astype(f32)


def pick(select, values):
    return dot_n(select.astype(bf16), values)


def pick_kernel(after_ref, ids_ref, values_ref, select_ref, rows_ref):
    select = select_of(ids_ref[...])
    select_ref[...] = select.astype(bf16)
    rows_ref[...] = pick(select, values_ref[...]).astype(bf16)


def norm_kernel(after_ref, ids_ref, values_ref, gain_ref, select_ref, rows_ref, *normed_refs):
    select = select_of(ids_ref[...])
    select_ref[...] = select.astype(bf16)
    rows = pick(select, values_ref[...])
    rows_ref[...] = rows.astype(bf16)
    inverse = lax.rsqrt(jnp.mean(rows * rows, axis=1, keepdims=True) + epsilon)
    normed = (rows * inverse * gain_ref[...]).astype(bf16)
    first = 0
    for normed_ref in normed_refs:
        last = first + normed_ref.shape[1]
        normed_ref[...] = normed[:, first:last]
        first = last


def front_call(after, ids, values, gain=None, cuts=0):
    tokens, width = values.shape
    capacity = tokens // 4
    more = [] if gain is None else [gain]
    return pl.pallas_call(
        pick_kernel if gain is None else norm_kernel,
        in_specs=[anywhere] + [in_vmem] * (2 + len(more)),
        out_specs=[in_vmem] * (2 + cuts),
        out_shape=[shape_of(capacity, tokens), shape_of(capacity, width)]
        + [shape_of(capacity, width // cuts) for _ in range(cuts)],
        compiler_params=params(8),
        cost_estimate=cost(0, 8 * values.size),
    )(after, ids, values, *more)


def act_kernel(rows_ref, weight_ref, own_ref, a_ref, b_ref, out_ref):
    total = own_ref[...].astype(f32) + a_ref[...].astype(f32) + b_ref[...].astype(f32)
    out_ref[...] = (rows_ref[...].astype(f32) + weight_ref[:, :1] * total).astype(bf16)


def act_call(rows, weight, own, a, b):
    return pl.pallas_call(
        act_kernel,
        in_specs=[in_vmem] * 5,
        out_specs=in_vmem,
        out_shape=shape_of(*rows.shape),
        compiler_params=params(6),
        cost_estimate=cost(0, 10 * rows.size),
    )(rows, weight, own, a, b)


def grad_kernel(rows_ref, above_ref, gain_ref, scale_ref, tilt_ref, own_ref, a_ref, b_ref, out_ref):
    width = rows_ref.shape[1]
    total = own_ref[...].astype(f32) + a_ref[...].astype(f32) + b_ref[...].astype(f32)
    rows = rows_ref[...].astype(f32)
    scale = scale_ref[:, :1].astype(bf16).astype(f32)
    cot = (total[:, :width] * scale + tilt_ref[...] * total[:, width : width + 1]) * gain_ref[...]
    inverse = lax.rsqrt(jnp.mean(rows * rows, axis=1, keepdims=True) + epsilon)
    along = jnp.mean(rows * cot, axis=1, keepdims=True) * (inverse * inverse * inverse)
    out_ref[...] = (above_ref[...].astype(f32) + (inverse * cot - rows * along)).astype(bf16)


def grad_call(rows, above, gain, scale, tilt, sums):
    return pl.pallas_call(
        grad_kernel,
        in_specs=[in_vmem] * (5 + len(sums)),
        out_specs=in_vmem,
        out_shape=shape_of(*rows.shape),
        compiler_params=params(16),
        cost_estimate=cost(0, 16 * rows.size),
    )(rows, above, gain, scale, tilt, *sums)


def place_kernel(select_ref, rows_ref, base_ref, out_ref):
    select = select_ref[...]
    one = jnp.ones((select.shape[0], 128), bf16)
    used = lax.dot_general(select, one, first_dims, preferred_element_type=f32)[:, :1] > 0
    for part in pieces_of(base_ref.shape[1], 6, 128):
        spread_rows = lax.dot_general(select, rows_ref[:, part], first_dims, preferred_element_type=f32)
        out_ref[:, part] = jnp.where(used, spread_rows.astype(bf16), base_ref[:, part])


def place_call(select, rows, base):
    return pl.pallas_call(
        place_kernel,
        in_specs=[in_vmem] * 3,
        out_specs=in_vmem,
        out_shape=shape_of(*base.shape),
        compiler_params=params(12),
        cost_estimate=cost(0, 4 * base.size),
    )(select, rows, base)


def route_kernel(after_ref, rows_ref, gain_ref, router_ref, ids_ref, weight_ref, *tilt_refs):
    ids, experts = ids_ref[...], router_ref.shape[0]
    select = select_of(ids).astype(bf16)
    rows = rows_ref[...].astype(f32)
    inverse = lax.rsqrt(jnp.mean(rows * rows, axis=1, keepdims=True) + epsilon)
    logits = lax.dot_general(
        rows * inverse * gain_ref[...], router_ref[...], last_dims, precision=highest, preferred_element_type=f32
    )
    expert = lax.broadcasted_iota(jnp.int32, (experts, ids.shape[1]), 0)
    first, second = (dot_t(select, (ids[k : k + 1] == expert).astype(bf16)) for k in (0, 1))
    share = jax.nn.sigmoid(jnp.sum((first - second) * logits, axis=1, keepdims=True))
    first_named, second_named = first[:, :1], second[:, :1]
    weight = share * first_named + (1.0 - share) * second_named
    weight_ref[...] = jnp.broadcast_to(weight, weight_ref.shape)
    for tilt_ref in tilt_refs:
        slant = share * (1.0 - share) * (first_named - second_named)
        tilt_ref[...] = jnp.dot(
            slant * (first - second), router_ref[...], precision=highest, preferred_element_type=f32
        )


def route_call(after, rows, gain, router_mat, ids, tilts):
    capacity, width = rows.shape
    return pl.pallas_call(
        route_kernel,
        in_specs=[anywhere] + [in_vmem] * 4,
        out_specs=[in_vmem] * (1 + tilts),
        out_shape=[shape_of(capacity, 128, f32)] + [shape_of(capacity, width, f32)] * tilts,
        compiler_params=params(20),
        cost_estimate=cost(0, 12 * rows.size),
    )(after, rows, gain, router_mat, ids)


def local(
    act_in, saved_in, grad_in, fwd_routes, bwd_routes, w_gate, w_up, w_down, router, norm_gain
):
    count = lax.axis_size("expert")
    gate, up, down = (pltpu.with_memory_space_constraint(array[0], pltpu.HBM) for array in (w_gate, w_up, w_down))
    router_mat = router[0].T
    fwd_ids, bwd_ids = fwd_routes[0].T, bwd_routes[0].T
    gather_f, gather_u, gather_h = Gather("f"), Gather("u"), Gather("h")
    scatter_o, scatter_r = Scatter("o"), Scatter("r")
    env = {"act_base": shifted(act_in[0], 1), "grad_base": shifted(grad_in[0], -1)}

    env["select_f"], env["rows_f"], normed_f = front_call(norm_gain, fwd_ids, act_in[0], norm_gain, 1)
    gather_f.begin(normed_f)

    def front_u(after):
        env["select_b"], rows = front_call(after, bwd_ids, grad_in[0])
        env["rows_u"] = rows
        gather_u.begin(rows)
        return (rows[:16, :128],)

    def front_b(after):
        _, env["rows_b"], normed = front_call(after, bwd_ids, saved_in[0], norm_gain, 1)
        gather_h.begin(normed)
        return (normed[:16, :128],)

    def shifts(select_f):
        env["select_f_there"], env["select_b_there"] = shifted(select_f, 1), shifted(env["select_b"], -1)
        return ()

    def route_f(select_f):
        return tuple(route_call(select_f, env["rows_f"], norm_gain, router_mat, fwd_ids, 0))

    def route_b(select_f):
        return tuple(route_call(select_f, env["rows_b"], norm_gain, router_mat, bwd_ids, 1))

    def load(name, weight):
        def does(after):
            env[name], flag = load_call(after, weight)
            return (flag,)

        return does

    def active(after):
        return (active_call(gather_f.held, env["gate"], env["up"]),)

    def outpart(active):
        parts = outpart_call(count, active, down)
        scatter_o.begin(parts)
        return (parts[0][0][:16, :128],)

    def back(after):
        return (back_call(gather_u.held, down),)

    def cots(back):
        return cots_call(gather_h.held, env["gate"], env["up"], back)

    def rowpart(gate_cot, up_cot, slope):
        parts = rowpart_call(count, gate_cot, up_cot, slope, env["gate"], up)
        scatter_r.begin(parts)
        env["renewed"] = list(parts)
        return ()

    def act_rows(weight_f):
        rows = act_call(env["rows_f"], weight_f, scatter_o.parts[0][0], *scatter_o.inbox)
        env["act_rows"] = shifted(rows, 1)
        return ()

    def act_place(select, rows, base):
        return (place_call(select, rows, base),)

    last = gather_u.steps - 1
    windows = [[(gather_f, step, 1)] for step in range(last + 1)]
    windows[-1].append((gather_u, 0, 2))
    for step in range(1, last):
        windows += [[(gather_h, step - 1, 2)], [(gather_u, step, 2)]]
    windows += [[(gather_h, last - 1, 2)], [(gather_u, last, 1), (scatter_o, 0, 1)]]
    windows += [[(gather_h, last, 1), (scatter_o, 1, 1)]]
    windows += [[(scatter_o, step, 1)] for step in range(2, last + 1)]
    windows += [[(scatter_r, step, 1)] for step in range(last + 1)]
    start = {(ring, step): k for k, transfers in enumerate(windows) for ring, step, _ in transfers}
    pieces = {}

    def put(window, needs, does, gives):
        pieces.setdefault(window, []).append((needs, does, gives))

    def nothing(*arrays):
        return ()

    f_done = start[gather_f, last] + 1
    h_done = start[gather_h, last] + 1
    out = start[scatter_o, last]
    put(0, ("select_f",), front_u, ("corner_u",))
    put(1, ("select_f",), front_b, ("corner_b",))
    put(1, ("select_f",), load("gate", gate), ("flag_g",))
    put(2, ("select_f",), load("up", up), ("flag_u",))
    put(f_done, ("select_f",), active, ("active",))
    put(f_done + 1, ("active",), outpart, ("corner_o",))
    put(h_done-1, ("act_base",), nothing, ())
    put(out+1, ("grad_base",), nothing, ())
    put(out+1, ("select_f",), shifts, ())
    put(h_done - 1, ("select_f",), back, ("back",))
    put(h_done, ("back",), cots, ("gate_cot", "up_cot", "slope"))
    put(h_done + 1, ("gate_cot", "up_cot", "slope"), rowpart, ())
    put(out + 1, ("select_f",), route_f, ("weight_f",))
    put(out + 2, ("weight_f",), act_rows, ())
    put(out + 3, ("select_f",), route_b, ("scale", "tilt"))
    put(out + 4, ("select_f_there", "act_rows", "act_base"), act_place, ("act_out",))
    run_windows(windows, pieces, env)

    sums = [scatter_r.parts[0][0], *scatter_r.inbox]
    grad_rows = grad_call(env["rows_b"], env["rows_u"], norm_gain, env["scale"], env["tilt"], sums)
    grad_out = place_call(env["select_b_there"], shifted(grad_rows, -1), env["grad_base"])
    return (env["act_out"][None], grad_out[None])


def solution(mesh):
    in_specs = (
        P("section", "expert", None),
        P("section", "expert", None),
        P("section", "expert", None),
        P("section", "expert", None),
        P("section", "expert", None),
        P("section", None, "expert"),
        P("section", None, "expert"),
        P("section", "expert", None),
        P("section", None, None),
        P("section", None),
    )
    out_specs = (P("section", "expert", None), P("section", "expert", None))
    return jax.shard_map(local, mesh=mesh, in_specs=in_specs, out_specs=out_specs, check_vma=False)
```

```python
import functools

import jax
import jax.numpy as jnp
from jax import lax
from jax.experimental import pallas as pl
from jax.experimental.pallas import tpu as pltpu
from jax.sharding import PartitionSpec as P

epsilon = 1e-05
highest = lax.Precision.HIGHEST
f32 = jnp.float32
bf16 = jnp.bfloat16
last_dims = (((1,), (1,)), ((), ()))
first_dims = (((0,), (0,)), ((), ()))
in_hbm = pl.BlockSpec(memory_space=pltpu.HBM)
anywhere = pl.BlockSpec(memory_space=pl.ANY)
in_vmem = pl.BlockSpec(memory_space=pltpu.VMEM)


def shape_of(rows, columns, dtype=bf16):
    return jax.ShapeDtypeStruct((rows, columns), dtype)


def params(mega):
    return pltpu.CompilerParams(vmem_limit_bytes=mega * 1024 * 1024)


def cost(flops, moved):
    return pl.CostEstimate(flops=int(flops), bytes_accessed=int(moved), transcendentals=0)


def dot_t(left, right):
    return lax.dot_general(left, right, last_dims, preferred_element_type=f32)


def dot_n(left, right):
    return jnp.dot(left, right, preferred_element_type=f32)


def hop(value, steps):
    count = lax.axis_size("expert")
    ring = list(range(0, count, 2)) + list(range(1, count, 2))[::-1]
    return lax.ppermute(value, "expert", [(ring[i], ring[(i + steps) % count]) for i in range(count)])


def shifted(value, steps):
    count = lax.axis_size("section")
    return lax.ppermute(value, "section", [(source, (source + steps) % count) for source in range(count)])


def halves(value):
    middle = value.shape[1] // 2
    return [value[:, :middle], value[:, middle:]]


class Ring:

    def __init__(self, name):
        self.name = name
        self.count = lax.axis_size("expert")
        self.full = (self.count - 1) // 2
        self.split = self.count % 2 == 0
        self.steps = self.full + self.split


class Gather(Ring):

    def begin(self, shard):
        self.held = [[shard]] + [None] * (self.count - 1)

    def send(self, step):
        ahead = self.held[-step % self.count][0]
        behind = self.held[step][0]
        if step == self.full:
            ahead, behind = halves(ahead)[0], halves(behind)[1]
        return [hop(ahead, 1), hop(behind, -1)]

    def receive(self, step, values):
        if step == self.full:
            self.held[step + 1] = values
        else:
            self.held[-1 - step], self.held[step + 1] = [values[0]], [values[1]]

    def sources(self, step):
        return [self.held[0]] if step == 0 else []


class Scatter(Ring):

    def begin(self, parts):
        self.parts = parts

    def send(self, step):
        far = self.steps - step
        if step > 0:
            ahead, behind = merge_call(self.parts[far][0], self.inbox[0], self.parts[-far][0], self.inbox[1])
        else:
            ahead, behind = self.parts[far][0], self.parts[-far][-1]
        return [hop(ahead, 1), hop(behind, -1)]

    def receive(self, step, values):
        self.inbox = values

    def sources(self, step):
        return [self.parts[self.steps]] + [self.parts[-self.steps]] * (1 - self.split) if step == 0 else []


def fence(arrays):
    return list(
        pl.pallas_call(
            lambda *refs: None,
            in_specs=[anywhere] * len(arrays),
            out_specs=[anywhere] * len(arrays),
            out_shape=[jax.ShapeDtypeStruct(array.shape, array.dtype) for array in arrays],
            compiler_params=params(1),
            cost_estimate=cost(0, 0),
            input_output_aliases={k: k for k in range(len(arrays))},
        )(*arrays)
    )


def run_windows(windows, pieces, env):
    flying, made = [], []
    for k, transfers in enumerate(windows):
        todo = pieces.get(k, [])
        names = list(made)
        for needs, _, _ in todo:
            names += [name for name in needs if name not in names]
        sources = env.pop("renewed", [])
        for ring, step, _ in transfers:
            sources += [held for held in ring.sources(step) if not any(held is other for other in sources)]
        landing = [flight for flight in flying if flight[2] <= k]
        flying = [flight for flight in flying if flight[2] > k]
        landed = [value for _, _, _, values in landing for value in values]
        passed = fence(landed + [env[name] for name in names] + [value for held in sources for value in held])
        for ring, step, _, values in landing:
            ring.receive(step, passed[: len(values)])
            passed = passed[len(values) :]
        for name in names:
            env[name] = passed.pop(0)
        for held in sources:
            held[:] = [passed.pop(0) for _ in held]
        with jax.named_scope(f"window_{k}"):
            flying += [(ring, step, k + stay, ring.send(step)) for ring, step, stay in transfers]
        made = []
        for needs, does, gives in todo:
            for name, value in zip(gives, does(*[env[name] for name in needs]), strict=True):
                env[name] = value
                made.append(name)
    for ring, step, _, values in flying:
        ring.receive(step, values)


def pieces_of(length, most, grain):
    for number in range(most, 1, -1):
        if length % (number * grain) == 0:
            size = length // number
            return [slice(k * size, (k + 1) * size) for k in range(number)]
    return [slice(0, length)]


def flat(held):
    return [value for shard in held for value in shard]


def row_copies(held_shape, shards, rows_ref, sems):
    side = rows_ref.shape[0] // len(held_shape)
    copies, at = [], 0
    for k, widths in enumerate(held_shape):
        first = 0
        for wide in widths:
            target = rows_ref.at[k * side : (k + 1) * side, first : first + wide]
            copies.append(pltpu.make_async_copy(shards[at], target, sems.at[at]))
            first, at = first + wide, at + 1
    return copies


def widths_of(held):
    return tuple(tuple(value.shape[1] for value in shard) for shard in held)


def start_all(*lists):
    for group in zip(*lists, strict=True):
        for copy in group:
            copy.start()


def merge_kernel(own_a_ref, value_a_ref, own_b_ref, value_b_ref, out_a_ref, out_b_ref):
    for own_ref, value_ref, out_ref, first in (
        (own_a_ref, value_a_ref, out_a_ref, 0),
        (own_b_ref, value_b_ref, out_b_ref, own_b_ref.shape[1] - value_b_ref.shape[1]),
    ):
        here = slice(first, first + value_ref.shape[1])
        if value_ref.shape != own_ref.shape:
            out_ref[...] = own_ref[...]
        out_ref[:, here] = (own_ref[:, here].astype(f32) + value_ref[...].astype(f32)).astype(bf16)


def merge_call(own_a, value_a, own_b, value_b):
    return pl.pallas_call(
        merge_kernel,
        in_specs=[in_vmem] * 4,
        out_specs=[in_vmem] * 2,
        out_shape=[shape_of(*own.shape) for own in (own_a, own_b)],
        compiler_params=params(4),
        cost_estimate=cost(0, 6 * own_a.size),
    )(own_a, value_a, own_b, value_b)


def load_kernel(after_ref, source, target, flag_ref, sems):
    copies = [
        pltpu.make_async_copy(source.at[part], target.at[part], sems.at[k])
        for k, part in enumerate(pieces_of(source.shape[0], 4, 128))
    ]
    start_all(copies)
    flag_ref[...] = jnp.zeros_like(flag_ref)
    for copy in copies:
        copy.wait()


def load_call(after, weight):
    return pl.pallas_call(
        load_kernel,
        in_specs=[anywhere, in_hbm],
        out_specs=[in_vmem, in_vmem],
        out_shape=[pltpu.VMEM(weight.shape, weight.dtype), shape_of(8, 128, f32)],
        scratch_shapes=[pltpu.SemaphoreType.DMA((4,))],
        compiler_params=params(1),
        cost_estimate=cost(0, 4 * weight.size),
    )(after, weight)


def back_kernel(held_shape, *refs):
    count = sum(len(widths) for widths in held_shape)
    shards, (down_ref, out_ref, rows_ref, row_sems) = refs[:count], refs[count:]
    parts = pieces_of(out_ref.shape[1], 4, 128)
    rows = row_copies(held_shape, shards, rows_ref, row_sems)
    start_all(rows)
    for copy in rows:
        copy.wait()
    for part in parts:
        out_ref[:, part] = dot_t(rows_ref[...], down_ref[part, :])


def back_call(held, down):
    count, side, width, hid = len(held), held[0][0].shape[0], sum(widths_of(held)[0]), down.shape[0]
    return pl.pallas_call(
        functools.partial(back_kernel, widths_of(held)),
        in_specs=[anywhere] * len(flat(held)) + [in_vmem],
        out_specs=in_vmem,
        out_shape=shape_of(count * side, hid, f32),
        scratch_shapes=[
            pltpu.VMEM((count * side, width), bf16),
            pltpu.SemaphoreType.DMA((len(flat(held)),)),
        ],
        compiler_params=params(8),
        cost_estimate=cost(2 * count * side * width * hid, 2 * width * (hid + count * side)),
    )(*flat(held), down)


def gate_up(held_shape, shards, gate_ref, up_ref, rows_ref, gate_sum, up_sum, up_w, row_sems, up_sems):
    parts = pieces_of(gate_ref.shape[0], 6, 128)
    rows = row_copies(held_shape, shards, rows_ref, row_sems)
    ups = [pltpu.make_async_copy(up_ref.at[part], up_w.at[part], up_sems.at[k]) for k, part in enumerate(parts)]
    start_all(rows)
    start_all(ups)
    for copy in rows:
        copy.wait()
    for k, part in enumerate(parts):
        product = dot_n(rows_ref[:, part], gate_ref[part, :])
        gate_sum[...] = product if k == 0 else gate_sum[...] + product
    for k, part in enumerate(parts):
        ups[k].wait()
        product = dot_n(rows_ref[:, part], up_w[part, :])
        up_sum[...] = product if k == 0 else up_sum[...] + product


def gate_up_scratch(copies, count, side, width, hid):
    return [
        pltpu.VMEM((count * side, width), bf16),
        pltpu.VMEM((count * side, hid), f32),
        pltpu.VMEM((count * side, hid), f32),
        pltpu.VMEM((width, hid), bf16),
        pltpu.SemaphoreType.DMA((copies,)),
        pltpu.SemaphoreType.DMA((6,)),
    ]


def gate_up_cost(count, side, width, hid):
    return cost(4 * count * side * width * hid, 2 * width * (2 * hid + count * side))


def active_kernel(held_shape, *refs):
    count = sum(len(widths) for widths in held_shape)
    shards, (gate_ref, up_ref, out_ref, *scratch) = refs[:count], refs[count:]
    gate_up(held_shape, shards, gate_ref, up_ref, *scratch)
    gate_pre = scratch[1][...]
    out_ref[...] = (gate_pre * jax.nn.sigmoid(gate_pre) * scratch[2][...]).astype(bf16)


def active_call(held, gate, up):
    count, side, width, hid = len(held), held[0][0].shape[0], sum(widths_of(held)[0]), gate.shape[1]
    return pl.pallas_call(
        functools.partial(active_kernel, widths_of(held)),
        in_specs=[anywhere] * len(flat(held)) + [in_vmem, in_hbm],
        out_specs=in_vmem,
        out_shape=shape_of(count * side, hid),
        scratch_shapes=gate_up_scratch(len(flat(held)), count, side, width, hid),
        compiler_params=params(24),
        cost_estimate=gate_up_cost(count, side, width, hid),
    )(*flat(held), gate, up)


def cots_kernel(held_shape, *refs):
    count = sum(len(widths) for widths in held_shape)
    shards, (gate_ref, up_ref, back_ref, gate_cot_ref, up_cot_ref, slope_ref, *scratch) = refs[:count], refs[count:]
    gate_up(held_shape, shards, gate_ref, up_ref, *scratch)
    gate_pre, up_pre = scratch[1][...], scratch[2][...]
    sig = jax.nn.sigmoid(gate_pre)
    silu = gate_pre * sig
    back = back_ref[...]
    active = (silu * up_pre).astype(bf16).astype(f32)
    slope_ref[...] = jnp.broadcast_to(jnp.sum(active * back, axis=1, keepdims=True), slope_ref.shape)
    gate_cot_ref[...] = (back * up_pre * sig * (1.0 + gate_pre * (1.0 - sig))).astype(bf16)
    up_cot_ref[...] = (back * silu).astype(bf16)


def cots_call(held, gate, up, back):
    count, side, width, hid = len(held), held[0][0].shape[0], sum(widths_of(held)[0]), gate.shape[1]
    return pl.pallas_call(
        functools.partial(cots_kernel, widths_of(held)),
        in_specs=[anywhere] * len(flat(held)) + [in_vmem, in_hbm, in_vmem],
        out_specs=[in_vmem] * 3,
        out_shape=[
            shape_of(count * side, hid),
            shape_of(count * side, hid),
            shape_of(count * side, 128, f32),
        ],
        scratch_shapes=gate_up_scratch(len(flat(held)), count, side, width, hid),
        compiler_params=params(26),
        cost_estimate=gate_up_cost(count, side, width, hid),
    )(*flat(held), gate, up, back)


def segments(count, width, extra):
    whole, pair = [(0, width + extra)], [(0, width // 2), (width // 2, width + extra)]
    return [pair if 2 * k == count else whole for k in range(count)]


def part_shapes(side, held):
    return [shape_of(side, last - first) for ranges in held for first, last in ranges]


def spread(made, held, first, value):
    side, last, at = value.shape[0] // len(held), first + value.shape[1], 0
    for k, ranges in enumerate(held):
        for low, high in ranges:
            begin, end = max(first, low), min(last, high)
            if begin < end:
                rows = value[k * side : (k + 1) * side, begin - first : end - first]
                made[at][:, begin - low : end - low] = rows
            at += 1


def send_out(made, out_refs, sems):
    copies = [
        pltpu.make_async_copy(source, target, sems.at[at])
        for at, (source, target) in enumerate(zip(made, out_refs, strict=True))
    ]
    start_all(copies)
    for copy in copies:
        copy.wait()


def made_scratch(shapes):
    return [pltpu.VMEM(shape.shape, shape.dtype) for shape in shapes] + [pltpu.SemaphoreType.DMA((len(shapes),))]


def regroup(held, arrays):
    arrays = list(arrays)
    return [[arrays.pop(0) for _ in ranges] for ranges in held]


def outpart_kernel(held, active_ref, down_ref, *refs):
    number = sum(len(ranges) for ranges in held)
    out_refs, made, (out_sems,) = refs[:number], refs[number : 2 * number], refs[2 * number :]
    width = down_ref.shape[1]
    parts = pieces_of(width, 6, 128)
    for part in parts:
        value = dot_n(active_ref[...], down_ref[:, part])
        spread(made, held, part.start, value.astype(bf16))
    send_out(made, out_refs, out_sems)


def outpart_call(count, active, down):
    rows, (hid, width) = active.shape[0], down.shape
    held = segments(count, width, 0)
    shapes = part_shapes(rows // count, held)
    arrays = pl.pallas_call(
        functools.partial(outpart_kernel, held),
        in_specs=[in_vmem] * 2,
        out_specs=[anywhere] * len(shapes),
        out_shape=shapes,
        scratch_shapes=made_scratch(shapes),
        compiler_params=params(6),
        cost_estimate=cost(2 * rows * width * hid, 2 * width * hid),
    )(active, down)
    return regroup(held, arrays)


def rowpart_kernel(held, gate_cot_ref, up_cot_ref, slope_ref, gate_ref, up_ref, *refs):
    out_refs, (up_w, up_sems) = refs[:-2], refs[-2:]
    width = gate_ref.shape[0]
    parts = pieces_of(width, 6, 128)

    ups = [pltpu.make_async_copy(up_ref.at[part], up_w.at[part], up_sems.at[k]) for k, part in enumerate(parts)]
    start_all(ups)
    spread(out_refs, held, width, slope_ref[...].astype(bf16))
    ahead = [dot_t(gate_cot_ref[...], gate_ref[part, :]) for part in parts[:2]]
    for k, part in enumerate(parts):
        ups[k].wait()
        value = ahead.pop(0) + dot_t(up_cot_ref[...], up_w[part, :])
        spread(out_refs, held, part.start, value.astype(bf16))
        if k + 2 < len(parts):
            ahead.append(dot_t(gate_cot_ref[...], gate_ref[parts[k + 2], :]))


def rowpart_call(count, gate_cot, up_cot, slope, gate, up):
    rows, (width, hid) = gate_cot.shape[0], gate.shape
    held = segments(count, width, slope.shape[1])
    shapes = part_shapes(rows // count, held)
    arrays = pl.pallas_call(
        functools.partial(rowpart_kernel, held),
        in_specs=[in_vmem] * 4 + [in_hbm],
        out_specs=[in_vmem] * len(shapes),
        out_shape=shapes,
        scratch_shapes=[pltpu.VMEM((width, hid), bf16), pltpu.SemaphoreType.DMA((6,))],
        compiler_params=params(20),
        cost_estimate=cost(4 * rows * width * hid, 4 * width * hid),
    )(gate_cot, up_cot, slope, gate, up)
    return regroup(held, arrays)


def select_of(ids):
    tokens = ids.shape[1]
    capacity = tokens // 4
    named = jnp.max((ids == 0).astype(f32), axis=0, keepdims=True)
    row = lax.broadcasted_iota(jnp.int32, (tokens, tokens), 0)
    column = lax.broadcasted_iota(jnp.int32, (tokens, tokens), 1)
    earlier = (row < column).astype(bf16)
    rank = dot_n(jnp.broadcast_to(named, (8, tokens)).astype(bf16), earlier)[:1]
    slot = jnp.where(named > 0, rank, float(capacity))
    places = lax.broadcasted_iota(jnp.int32, (capacity, tokens), 0).astype(f32)
    return (slot == places).astype(f32)


def pick(select, values):
    return dot_n(select.astype(bf16), values)


def front_kernel(after_ref, ids_hbm, values_hbm, gain_hbm, *refs):
    select_ref, rows_ref, *normed_refs = refs[:-4]
    ids_ref, values_ref, gain_ref, sems = refs[-4:]
    copies = [
        pltpu.make_async_copy(source, target, sems.at[k])
        for k, (source, target) in enumerate(
            ((ids_hbm, ids_ref), (values_hbm, values_ref), (gain_hbm, gain_ref))
        )
    ]
    start_all(copies)
    copies[0].wait()
    select = select_of(ids_ref[...])
    select_ref[...] = select.astype(bf16)
    copies[1].wait()
    rows = pick(select, values_ref[...])
    rows_ref[...] = rows.astype(bf16)
    copies[2].wait()
    for normed_ref in normed_refs:
        inverse = lax.rsqrt(jnp.mean(rows * rows, axis=1, keepdims=True) + epsilon)
        normed_ref[...] = (rows * inverse * gain_ref[...]).astype(bf16)


def front_call(after, ids, values, gain, normed):
    tokens, width = values.shape
    capacity = tokens // 4
    ids, values, gain = (pltpu.with_memory_space_constraint(array, pltpu.HBM) for array in (ids, values, gain))
    return pl.pallas_call(
        front_kernel,
        in_specs=[anywhere] + [in_hbm] * 3,
        out_specs=[in_vmem] * (2 + normed),
        out_shape=[shape_of(capacity, tokens)] + [shape_of(capacity, width)] * (1 + normed),
        scratch_shapes=[
            pltpu.VMEM(ids.shape, ids.dtype),
            pltpu.VMEM(values.shape, values.dtype),
            pltpu.VMEM(gain.shape, gain.dtype),
            pltpu.SemaphoreType.DMA((3,)),
        ],
        compiler_params=params(8),
        cost_estimate=cost(0, 8 * values.size),
    )(after, ids, values, gain)


def act_kernel(rows_ref, weight_ref, own_ref, a_ref, b_ref, out_ref):
    total = own_ref[...].astype(f32) + a_ref[...].astype(f32) + b_ref[...].astype(f32)
    out_ref[...] = (rows_ref[...].astype(f32) + weight_ref[:, :1] * total).astype(bf16)


def act_call(rows, weight, own, a, b):
    return pl.pallas_call(
        act_kernel,
        in_specs=[in_vmem] * 5,
        out_specs=in_vmem,
        out_shape=shape_of(*rows.shape),
        compiler_params=params(6),
        cost_estimate=cost(0, 10 * rows.size),
    )(rows, weight, own, a, b)


def grad_kernel(rows_ref, above_ref, gain_ref, scale_ref, tilt_ref, own_ref, a_ref, b_ref, out_ref):
    width = rows_ref.shape[1]
    total = own_ref[...].astype(f32) + a_ref[...].astype(f32) + b_ref[...].astype(f32)
    rows = rows_ref[...].astype(f32)
    scale = scale_ref[:, :1].astype(bf16).astype(f32)
    cot = (total[:, :width] * scale + tilt_ref[...] * total[:, width : width + 1]) * gain_ref[...]
    inverse = lax.rsqrt(jnp.mean(rows * rows, axis=1, keepdims=True) + epsilon)
    along = jnp.mean(rows * cot, axis=1, keepdims=True) * (inverse * inverse * inverse)
    out_ref[...] = (above_ref[...].astype(f32) + (inverse * cot - rows * along)).astype(bf16)


def grad_call(rows, above, gain, scale, tilt, sums):
    return pl.pallas_call(
        grad_kernel,
        in_specs=[in_vmem] * (5 + len(sums)),
        out_specs=in_vmem,
        out_shape=shape_of(*rows.shape),
        compiler_params=params(16),
        cost_estimate=cost(0, 16 * rows.size),
    )(rows, above, gain, scale, tilt, *sums)


def place_kernel(select_ref, rows_ref, base_ref, out_ref):
    select = select_ref[...]
    one = jnp.ones((select.shape[0], 128), bf16)
    used = lax.dot_general(select, one, first_dims, preferred_element_type=f32)[:, :1] > 0
    for part in pieces_of(base_ref.shape[1], 6, 128):
        spread_rows = lax.dot_general(select, rows_ref[:, part], first_dims, preferred_element_type=f32)
        out_ref[:, part] = jnp.where(used, spread_rows.astype(bf16), base_ref[:, part])


def place_call(select, rows, base):
    return pl.pallas_call(
        place_kernel,
        in_specs=[in_vmem] * 3,
        out_specs=in_vmem,
        out_shape=shape_of(*base.shape),
        compiler_params=params(12),
        cost_estimate=cost(0, 4 * base.size),
    )(select, rows, base)


def route_kernel(after_ref, rows_ref, gain_ref, router_ref, ids_ref, weight_ref, *tilt_refs):
    ids, experts = ids_ref[...], router_ref.shape[0]
    select = select_of(ids).astype(bf16)
    rows = rows_ref[...].astype(f32)
    inverse = lax.rsqrt(jnp.mean(rows * rows, axis=1, keepdims=True) + epsilon)
    logits = lax.dot_general(
        rows * inverse * gain_ref[...], router_ref[...], last_dims, precision=highest, preferred_element_type=f32
    )
    expert = lax.broadcasted_iota(jnp.int32, (experts, ids.shape[1]), 0)
    first, second = (dot_t(select, (ids[k : k + 1] == expert).astype(bf16)) for k in (0, 1))
    share = jax.nn.sigmoid(jnp.sum((first - second) * logits, axis=1, keepdims=True))
    first_named, second_named = first[:, :1], second[:, :1]
    weight = share * first_named + (1.0 - share) * second_named
    weight_ref[...] = jnp.broadcast_to(weight, weight_ref.shape)
    for tilt_ref in tilt_refs:
        slant = share * (1.0 - share) * (first_named - second_named)
        tilt_ref[...] = jnp.dot(
            slant * (first - second), router_ref[...], precision=highest, preferred_element_type=f32
        )


def route_call(after, rows, gain, router_mat, ids, tilts):
    capacity, width = rows.shape
    return pl.pallas_call(
        route_kernel,
        in_specs=[anywhere] + [in_vmem] * 4,
        out_specs=[in_vmem] * (1 + tilts),
        out_shape=[shape_of(capacity, 128, f32)] + [shape_of(capacity, width, f32)] * tilts,
        compiler_params=params(20),
        cost_estimate=cost(0, 12 * rows.size),
    )(after, rows, gain, router_mat, ids)


def local(
    act_in, saved_in, grad_in, fwd_routes, bwd_routes, w_gate, w_up, w_down, router, norm_gain
):
    count = lax.axis_size("expert")
    gate, up, down = (pltpu.with_memory_space_constraint(array[0], pltpu.HBM) for array in (w_gate, w_up, w_down))
    router_mat = router[0].T
    fwd_ids, bwd_ids = fwd_routes[0].T, bwd_routes[0].T
    gather_f, gather_u, gather_h = Gather("f"), Gather("u"), Gather("h")
    scatter_o, scatter_r = Scatter("o"), Scatter("r")
    env = {"act_base": shifted(act_in[0], 1), "grad_base": shifted(grad_in[0], -1)}

    env["select_f"], env["rows_f"], normed_f = front_call(norm_gain, fwd_ids, act_in[0], norm_gain, 1)
    gather_f.begin(normed_f)

    def front_u(after):
        env["select_b"], rows = front_call(after, bwd_ids, grad_in[0], norm_gain, 0)
        env["rows_u"] = rows
        gather_u.begin(rows)
        return (rows[:16, :128],)

    def front_b(after):
        _, env["rows_b"], normed = front_call(after, bwd_ids, saved_in[0], norm_gain, 1)
        gather_h.begin(normed)
        return (normed[:16, :128],)

    def shifts(select_f):
        env["select_f_there"], env["select_b_there"] = shifted(select_f, 1), shifted(env["select_b"], -1)
        return ()

    def route_f(select_f):
        return tuple(route_call(select_f, env["rows_f"], norm_gain, router_mat, fwd_ids, 0))

    def route_b(select_f):
        return tuple(route_call(select_f, env["rows_b"], norm_gain, router_mat, bwd_ids, 1))

    def load(name, weight):
        def does(after):
            env[name], flag = load_call(after, weight)
            return (flag,)

        return does

    def active(after):
        return (active_call(gather_f.held, env["gate"], up),)

    def outpart(active):
        parts = outpart_call(count, active, env["down"])
        scatter_o.begin(parts)
        return (parts[0][0][:16, :128],)

    def back(after):
        return (back_call(gather_u.held, env["down"]),)

    def cots(back):
        return cots_call(gather_h.held, env["gate"], up, back)

    def rowpart(gate_cot, up_cot, slope):
        parts = rowpart_call(count, gate_cot, up_cot, slope, env["gate"], up)
        scatter_r.begin(parts)
        env["renewed"] = list(parts)
        return ()

    def act_rows(weight_f):
        rows = act_call(env["rows_f"], weight_f, scatter_o.parts[0][0], *scatter_o.inbox)
        env["act_rows"] = shifted(rows, 1)
        return ()

    def act_place(select, rows, base, other):
        return (place_call(select, rows, base),)

    last = gather_u.steps - 1
    turns = []
    for step in range(last):
        turns += [(gather_f, step), (gather_u, step) if step + 1 < last else (gather_h, 0)]
    turns += [(gather_f, last), (gather_u, last - 1), (gather_h, 1), (gather_u, last)]
    turns += [(gather_h, step) for step in range(2, last)]
    windows = [[turn] for turn in turns]
    windows += [[(scatter_o, 0)], [(gather_h, last), (scatter_o, 1)]]
    windows += [[(scatter_o, step)] for step in range(2, last + 1)]
    windows += [[(scatter_r, step)] for step in range(last + 1)]
    start = {turn: k for k, turns in enumerate(windows) for turn in turns}

    def stay(ring, step):
        return min(2, start.get((ring, step + 1), start[ring, step] + 2) - start[ring, step])

    windows = [[(ring, step, stay(ring, step)) for ring, step in turns] for turns in windows]
    windows[start[gather_h, last]] = [(gather_h, last, 1), (scatter_o, 1, 1)]
    windows[start[scatter_o, last]] = [(scatter_o, last, 1)]
    pieces = {}

    def put(window, needs, does, gives):
        pieces.setdefault(window, []).append((needs, does, gives))

    def nothing(*arrays):
        return ()

    f_done = start[gather_f, last] + 2
    h_done = start[gather_h, last] + 1
    out = start[scatter_o, last]
    put(0, ("select_f",), front_u, ("corner_u",))
    put(1, ("select_f",), front_b, ("corner_b",))
    put(2, ("select_f",), load("gate", gate), ("flag_g",))
    put(3, ("select_f",), load("down", down), ("flag_d",))
    put(f_done, ("select_f",), active, ("active",))
    put(f_done + 1, ("active",), outpart, ("corner_o",))
    put(h_done-3, ("act_base",), nothing, ())
    put(out+1, ("grad_base",), nothing, ())
    put(h_done - 2, ("select_f",), back, ("back",))
    put(h_done, ("back",), cots, ("gate_cot", "up_cot", "slope"))
    put(h_done + 1, ("gate_cot", "up_cot", "slope"), rowpart, ())
    put(out + 1, ("select_f",), shifts, ())
    put(out + 1, ("select_f",), route_f, ("weight_f",))
    put(out + 2, ("weight_f",), act_rows, ())
    put(out + 3, ("select_f",), route_b, ("scale", "tilt"))
    put(out + 4, ("select_f_there", "act_rows", "act_base", "select_b_there"), act_place, ("act_out",))
    run_windows(windows, pieces, env)

    sums = [scatter_r.parts[0][0], *scatter_r.inbox]
    grad_rows = grad_call(env["rows_b"], env["rows_u"], norm_gain, env["scale"], env["tilt"], sums)
    grad_out = place_call(env["select_b_there"], shifted(grad_rows, -1), env["grad_base"])
    return (env["act_out"][None], grad_out[None])


def solution(mesh):
    in_specs = (
        P("section", "expert", None),
        P("section", "expert", None),
        P("section", "expert", None),
        P("section", "expert", None),
        P("section", "expert", None),
        P("section", None, "expert"),
        P("section", None, "expert"),
        P("section", "expert", None),
        P("section", None, None),
        P("section", None),
    )
    out_specs = (P("section", "expert", None), P("section", "expert", None))
    return jax.shard_map(local, mesh=mesh, in_specs=in_specs, out_specs=out_specs, check_vma=False)
```

```python
import functools

import jax
import jax.numpy as jnp
from jax import lax
from jax.experimental import pallas as pl
from jax.experimental.pallas import tpu as pltpu
from jax.sharding import PartitionSpec as P

epsilon = 1e-05
highest = lax.Precision.HIGHEST
f32 = jnp.float32
bf16 = jnp.bfloat16
last_dims = (((1,), (1,)), ((), ()))
first_dims = (((0,), (0,)), ((), ()))
in_hbm = pl.BlockSpec(memory_space=pltpu.HBM)
anywhere = pl.BlockSpec(memory_space=pl.ANY)
in_vmem = pl.BlockSpec(memory_space=pltpu.VMEM)


def shape_of(rows, columns, dtype=bf16):
    return jax.ShapeDtypeStruct((rows, columns), dtype)


def params(mega):
    return pltpu.CompilerParams(vmem_limit_bytes=mega * 1024 * 1024)


def cost(flops, moved):
    return pl.CostEstimate(flops=int(flops), bytes_accessed=int(moved), transcendentals=0)


def dot_t(left, right):
    return lax.dot_general(left, right, last_dims, preferred_element_type=f32)


def dot_n(left, right):
    return jnp.dot(left, right, preferred_element_type=f32)


def hop(value, steps):
    count = lax.axis_size("expert")
    ring = list(range(0, count, 2)) + list(range(1, count, 2))[::-1]
    return lax.ppermute(value, "expert", [(ring[i], ring[(i + steps) % count]) for i in range(count)])


def shifted(value, steps):
    count = lax.axis_size("section")
    return lax.ppermute(value, "section", [(source, (source + steps) % count) for source in range(count)])


def halves(value):
    middle = value.shape[1] // 2
    return [value[:, :middle], value[:, middle:]]


class Ring:

    def __init__(self, name):
        self.name = name
        self.count = lax.axis_size("expert")
        self.full = (self.count - 1) // 2
        self.split = self.count % 2 == 0
        self.steps = self.full + self.split


class Gather(Ring):

    def begin(self, shard):
        self.held = [[shard]] + [None] * (self.count - 1)

    def send(self, step):
        ahead = self.held[-step % self.count][0]
        behind = self.held[step][0]
        if step == self.full:
            ahead, behind = halves(ahead)[0], halves(behind)[1]
        return [hop(ahead, 1), hop(behind, -1)]

    def receive(self, step, values):
        if step == self.full:
            self.held[step + 1] = values
        else:
            self.held[-1 - step], self.held[step + 1] = [values[0]], [values[1]]

    def sources(self, step):
        return [self.held[0]] if step == 0 else []


class Scatter(Ring):

    def begin(self, parts):
        self.parts = parts

    def send(self, step):
        far = self.steps - step
        if step > 0:
            ahead, behind = merge_call(self.parts[far][0], self.inbox[0], self.parts[-far][0], self.inbox[1])
        else:
            ahead, behind = self.parts[far][0], self.parts[-far][-1]
        return [hop(ahead, 1), hop(behind, -1)]

    def receive(self, step, values):
        self.inbox = values

    def sources(self, step):
        return [self.parts[self.steps]] + [self.parts[-self.steps]] * (1 - self.split) if step == 0 else []


def fence(arrays):
    return list(
        pl.pallas_call(
            lambda *refs: None,
            in_specs=[anywhere] * len(arrays),
            out_specs=[anywhere] * len(arrays),
            out_shape=[jax.ShapeDtypeStruct(array.shape, array.dtype) for array in arrays],
            compiler_params=params(1),
            cost_estimate=cost(0, 0),
            input_output_aliases={k: k for k in range(len(arrays))},
        )(*arrays)
    )


def run_windows(windows, pieces, env):
    flying, made = [], []
    for k, transfers in enumerate(windows):
        todo = pieces.get(k, [])
        names = list(made)
        for needs, _, _ in todo:
            names += [name for name in needs if name not in names]
        sources = env.pop("renewed", [])
        for ring, step, _ in transfers:
            sources += [held for held in ring.sources(step) if not any(held is other for other in sources)]
        landing = [flight for flight in flying if flight[2] <= k]
        flying = [flight for flight in flying if flight[2] > k]
        landed = [value for _, _, _, values in landing for value in values]
        passed = fence(landed + [env[name] for name in names] + [value for held in sources for value in held])
        for ring, step, _, values in landing:
            ring.receive(step, passed[: len(values)])
            passed = passed[len(values) :]
        for name in names:
            env[name] = passed.pop(0)
        for held in sources:
            held[:] = [passed.pop(0) for _ in held]
        with jax.named_scope(f"window_{k}"):
            flying += [(ring, step, k + stay, ring.send(step)) for ring, step, stay in transfers]
        made = []
        for needs, does, gives in todo:
            for name, value in zip(gives, does(*[env[name] for name in needs]), strict=True):
                env[name] = value
                made.append(name)
    for ring, step, _, values in flying:
        ring.receive(step, values)


def pieces_of(length, most, grain):
    for number in range(most, 1, -1):
        if length % (number * grain) == 0:
            size = length // number
            return [slice(k * size, (k + 1) * size) for k in range(number)]
    return [slice(0, length)]


def flat(held):
    return [value for shard in held for value in shard]


def row_copies(held_shape, shards, rows_ref, sems):
    side = rows_ref.shape[0] // len(held_shape)
    copies, at = [], 0
    for k, widths in enumerate(held_shape):
        first = 0
        for wide in widths:
            target = rows_ref.at[k * side : (k + 1) * side, first : first + wide]
            copies.append(pltpu.make_async_copy(shards[at], target, sems.at[at]))
            first, at = first + wide, at + 1
    return copies


def widths_of(held):
    return tuple(tuple(value.shape[1] for value in shard) for shard in held)


def start_all(*lists):
    for group in zip(*lists, strict=True):
        for copy in group:
            copy.start()


def merge_kernel(own_a_ref, value_a_ref, own_b_ref, value_b_ref, out_a_ref, out_b_ref):
    for own_ref, value_ref, out_ref, first in (
        (own_a_ref, value_a_ref, out_a_ref, 0),
        (own_b_ref, value_b_ref, out_b_ref, own_b_ref.shape[1] - value_b_ref.shape[1]),
    ):
        here = slice(first, first + value_ref.shape[1])
        if value_ref.shape != own_ref.shape:
            out_ref[...] = own_ref[...]
        out_ref[:, here] = (own_ref[:, here].astype(f32) + value_ref[...].astype(f32)).astype(bf16)


def merge_call(own_a, value_a, own_b, value_b):
    return pl.pallas_call(
        merge_kernel,
        in_specs=[in_vmem] * 4,
        out_specs=[in_vmem] * 2,
        out_shape=[shape_of(*own.shape) for own in (own_a, own_b)],
        compiler_params=params(4),
        cost_estimate=cost(0, 6 * own_a.size),
    )(own_a, value_a, own_b, value_b)


def load_kernel(after_ref, source, target, flag_ref, sems):
    copies = [
        pltpu.make_async_copy(source.at[part], target.at[part], sems.at[k])
        for k, part in enumerate(pieces_of(source.shape[0], 4, 128))
    ]
    start_all(copies)
    flag_ref[...] = jnp.zeros_like(flag_ref)
    for copy in copies:
        copy.wait()


def load_call(after, weight):
    return pl.pallas_call(
        load_kernel,
        in_specs=[anywhere, in_hbm],
        out_specs=[in_vmem, in_vmem],
        out_shape=[pltpu.VMEM(weight.shape, weight.dtype), shape_of(8, 128, f32)],
        scratch_shapes=[pltpu.SemaphoreType.DMA((4,))],
        compiler_params=params(1),
        cost_estimate=cost(0, 4 * weight.size),
    )(after, weight)


def back_kernel(held_shape, *refs):
    count = sum(len(widths) for widths in held_shape)
    shards, (down_ref, out_ref, rows_ref, row_sems) = refs[:count], refs[count:]
    parts = pieces_of(out_ref.shape[1], 4, 128)
    rows = row_copies(held_shape, shards, rows_ref, row_sems)
    start_all(rows)
    for copy in rows:
        copy.wait()
    for part in parts:
        out_ref[:, part] = dot_t(rows_ref[...], down_ref[part, :])


def back_call(held, down):
    count, side, width, hid = len(held), held[0][0].shape[0], sum(widths_of(held)[0]), down.shape[0]
    return pl.pallas_call(
        functools.partial(back_kernel, widths_of(held)),
        in_specs=[anywhere] * len(flat(held)) + [in_vmem],
        out_specs=in_vmem,
        out_shape=shape_of(count * side, hid, f32),
        scratch_shapes=[
            pltpu.VMEM((count * side, width), bf16),
            pltpu.SemaphoreType.DMA((len(flat(held)),)),
        ],
        compiler_params=params(8),
        cost_estimate=cost(2 * count * side * width * hid, 2 * width * (hid + count * side)),
    )(*flat(held), down)


def gate_up(held_shape, shards, gate_ref, up_ref, rows_ref, gate_sum, up_sum, up_w, row_sems, up_sems):
    parts = pieces_of(gate_ref.shape[0], 6, 128)
    rows = row_copies(held_shape, shards, rows_ref, row_sems)
    ups = [pltpu.make_async_copy(up_ref.at[part], up_w.at[part], up_sems.at[k]) for k, part in enumerate(parts)]
    start_all(rows)
    start_all(ups)
    for copy in rows:
        copy.wait()
    for k, part in enumerate(parts):
        product = dot_n(rows_ref[:, part], gate_ref[part, :])
        gate_sum[...] = product if k == 0 else gate_sum[...] + product
    for k, part in enumerate(parts):
        ups[k].wait()
        product = dot_n(rows_ref[:, part], up_w[part, :])
        up_sum[...] = product if k == 0 else up_sum[...] + product


def gate_up_held(held_shape, shards, gate_ref, up_ref, rows_ref, gate_sum, up_sum, row_sems):
    rows = row_copies(held_shape, shards, rows_ref, row_sems)
    start_all(rows)
    for copy in rows:
        copy.wait()
    for k, part in enumerate(pieces_of(gate_ref.shape[0], 6, 128)):
        for weight, total in ((gate_ref, gate_sum), (up_ref, up_sum)):
            product = dot_n(rows_ref[:, part], weight[part, :])
            total[...] = product if k == 0 else total[...] + product


def gate_up_scratch(copies, count, side, width, hid, held=False):
    sums = [pltpu.VMEM((count * side, hid), f32)] * 2
    loads = [] if held else [pltpu.VMEM((width, hid), bf16)]
    sems = [pltpu.SemaphoreType.DMA((copies,))] + [pltpu.SemaphoreType.DMA((6,))] * (not held)
    return [pltpu.VMEM((count * side, width), bf16), *sums, *loads, *sems]


def gate_up_cost(count, side, width, hid):
    return cost(4 * count * side * width * hid, 2 * width * (2 * hid + count * side))


def active_kernel(held_shape, *refs):
    count = sum(len(widths) for widths in held_shape)
    shards, (gate_ref, up_ref, out_ref, *scratch) = refs[:count], refs[count:]
    gate_up(held_shape, shards, gate_ref, up_ref, *scratch)
    gate_pre = scratch[1][...]
    out_ref[...] = (gate_pre * jax.nn.sigmoid(gate_pre) * scratch[2][...]).astype(bf16)


def active_call(held, gate, up):
    count, side, width, hid = len(held), held[0][0].shape[0], sum(widths_of(held)[0]), gate.shape[1]
    return pl.pallas_call(
        functools.partial(active_kernel, widths_of(held)),
        in_specs=[anywhere] * len(flat(held)) + [in_vmem, in_hbm],
        out_specs=in_vmem,
        out_shape=shape_of(count * side, hid),
        scratch_shapes=gate_up_scratch(len(flat(held)), count, side, width, hid),
        compiler_params=params(24),
        cost_estimate=gate_up_cost(count, side, width, hid),
    )(*flat(held), gate, up)


def cots_kernel(held_shape, *refs):
    count = sum(len(widths) for widths in held_shape)
    shards, (gate_ref, up_ref, back_ref, gate_cot_ref, up_cot_ref, slope_ref, *scratch) = refs[:count], refs[count:]
    gate_up_held(held_shape, shards, gate_ref, up_ref, *scratch)
    gate_pre, up_pre = scratch[1][...], scratch[2][...]
    sig = jax.nn.sigmoid(gate_pre)
    silu = gate_pre * sig
    back = back_ref[...]
    active = (silu * up_pre).astype(bf16).astype(f32)
    slope_ref[...] = jnp.broadcast_to(jnp.sum(active * back, axis=1, keepdims=True), slope_ref.shape)
    gate_cot_ref[...] = (back * up_pre * sig * (1.0 + gate_pre * (1.0 - sig))).astype(bf16)
    up_cot_ref[...] = (back * silu).astype(bf16)


def cots_call(held, gate, up, back):
    count, side, width, hid = len(held), held[0][0].shape[0], sum(widths_of(held)[0]), gate.shape[1]
    return pl.pallas_call(
        functools.partial(cots_kernel, widths_of(held)),
        in_specs=[anywhere] * len(flat(held)) + [in_vmem] * 3,
        out_specs=[in_vmem] * 3,
        out_shape=[
            shape_of(count * side, hid),
            shape_of(count * side, hid),
            shape_of(count * side, 128, f32),
        ],
        scratch_shapes=gate_up_scratch(len(flat(held)), count, side, width, hid, True),
        compiler_params=params(14),
        cost_estimate=gate_up_cost(count, side, width, hid),
    )(*flat(held), gate, up, back)


def segments(count, width, extra):
    whole, pair = [(0, width + extra)], [(0, width // 2), (width // 2, width + extra)]
    return [pair if 2 * k == count else whole for k in range(count)]


def part_shapes(side, held):
    return [shape_of(side, last - first) for ranges in held for first, last in ranges]


def spread(made, held, first, value):
    side, last, at = value.shape[0] // len(held), first + value.shape[1], 0
    for k, ranges in enumerate(held):
        for low, high in ranges:
            begin, end = max(first, low), min(last, high)
            if begin < end:
                rows = value[k * side : (k + 1) * side, begin - first : end - first]
                made[at][:, begin - low : end - low] = rows
            at += 1


def send_out(made, out_refs, sems):
    copies = [
        pltpu.make_async_copy(source, target, sems.at[at])
        for at, (source, target) in enumerate(zip(made, out_refs, strict=True))
    ]
    start_all(copies)
    for copy in copies:
        copy.wait()


def made_scratch(shapes):
    return [pltpu.VMEM(shape.shape, shape.dtype) for shape in shapes] + [pltpu.SemaphoreType.DMA((len(shapes),))]


def regroup(held, arrays):
    arrays = list(arrays)
    return [[arrays.pop(0) for _ in ranges] for ranges in held]


def outpart_kernel(held, active_ref, down_ref, *refs):
    number = sum(len(ranges) for ranges in held)
    out_refs, made, (out_sems,) = refs[:number], refs[number : 2 * number], refs[2 * number :]
    width = down_ref.shape[1]
    parts = pieces_of(width, 6, 128)
    for part in parts:
        value = dot_n(active_ref[...], down_ref[:, part])
        spread(made, held, part.start, value.astype(bf16))
    send_out(made, out_refs, out_sems)


def outpart_call(count, active, down):
    rows, (hid, width) = active.shape[0], down.shape
    held = segments(count, width, 0)
    shapes = part_shapes(rows // count, held)
    arrays = pl.pallas_call(
        functools.partial(outpart_kernel, held),
        in_specs=[in_vmem] * 2,
        out_specs=[anywhere] * len(shapes),
        out_shape=shapes,
        scratch_shapes=made_scratch(shapes),
        compiler_params=params(6),
        cost_estimate=cost(2 * rows * width * hid, 2 * width * hid),
    )(active, down)
    return regroup(held, arrays)


def rowpart_kernel(held, gate_cot_ref, up_cot_ref, slope_ref, gate_ref, up_ref, *out_refs):
    width = gate_ref.shape[0]
    parts = pieces_of(width, 6, 128)

    spread(out_refs, held, width, slope_ref[...].astype(bf16))
    for part in parts:
        value = dot_t(gate_cot_ref[...], gate_ref[part, :]) + dot_t(up_cot_ref[...], up_ref[part, :])
        spread(out_refs, held, part.start, value.astype(bf16))


def rowpart_call(count, gate_cot, up_cot, slope, gate, up):
    rows, (width, hid) = gate_cot.shape[0], gate.shape
    held = segments(count, width, slope.shape[1])
    shapes = part_shapes(rows // count, held)
    arrays = pl.pallas_call(
        functools.partial(rowpart_kernel, held),
        in_specs=[in_vmem] * 5,
        out_specs=[in_vmem] * len(shapes),
        out_shape=shapes,
        compiler_params=params(6),
        cost_estimate=cost(4 * rows * width * hid, 4 * width * hid),
    )(gate_cot, up_cot, slope, gate, up)
    return regroup(held, arrays)


def select_of(ids):
    tokens = ids.shape[1]
    capacity = tokens // 4
    named = jnp.max((ids == 0).astype(f32), axis=0, keepdims=True)
    row = lax.broadcasted_iota(jnp.int32, (tokens, tokens), 0)
    column = lax.broadcasted_iota(jnp.int32, (tokens, tokens), 1)
    earlier = (row < column).astype(bf16)
    rank = dot_n(jnp.broadcast_to(named, (8, tokens)).astype(bf16), earlier)[:1]
    slot = jnp.where(named > 0, rank, float(capacity))
    places = lax.broadcasted_iota(jnp.int32, (capacity, tokens), 0).astype(f32)
    return (slot == places).astype(f32)


def pick(select, values):
    return dot_n(select.astype(bf16), values)


def front_kernel(after_ref, ids_hbm, values_hbm, gain_hbm, *refs):
    select_ref, rows_ref, *normed_refs = refs[:-4]
    ids_ref, values_ref, gain_ref, sems = refs[-4:]
    copies = [
        pltpu.make_async_copy(source, target, sems.at[k])
        for k, (source, target) in enumerate(
            ((ids_hbm, ids_ref), (values_hbm, values_ref), (gain_hbm, gain_ref))
        )
    ]
    start_all(copies)
    copies[0].wait()
    select = select_of(ids_ref[...])
    select_ref[...] = select.astype(bf16)
    copies[1].wait()
    rows = pick(select, values_ref[...])
    rows_ref[...] = rows.astype(bf16)
    copies[2].wait()
    for normed_ref in normed_refs:
        inverse = lax.rsqrt(jnp.mean(rows * rows, axis=1, keepdims=True) + epsilon)
        normed_ref[...] = (rows * inverse * gain_ref[...]).astype(bf16)


def front_call(after, ids, values, gain, normed):
    tokens, width = values.shape
    capacity = tokens // 4
    ids, values, gain = (pltpu.with_memory_space_constraint(array, pltpu.HBM) for array in (ids, values, gain))
    return pl.pallas_call(
        front_kernel,
        in_specs=[anywhere] + [in_hbm] * 3,
        out_specs=[in_vmem] * (2 + normed),
        out_shape=[shape_of(capacity, tokens)] + [shape_of(capacity, width)] * (1 + normed),
        scratch_shapes=[
            pltpu.VMEM(ids.shape, ids.dtype),
            pltpu.VMEM(values.shape, values.dtype),
            pltpu.VMEM(gain.shape, gain.dtype),
            pltpu.SemaphoreType.DMA((3,)),
        ],
        compiler_params=params(8),
        cost_estimate=cost(0, 8 * values.size),
    )(after, ids, values, gain)


def act_kernel(rows_ref, weight_ref, own_ref, a_ref, b_ref, out_ref):
    total = own_ref[...].astype(f32) + a_ref[...].astype(f32) + b_ref[...].astype(f32)
    out_ref[...] = (rows_ref[...].astype(f32) + weight_ref[:, :1] * total).astype(bf16)


def act_call(rows, weight, own, a, b):
    return pl.pallas_call(
        act_kernel,
        in_specs=[in_vmem] * 5,
        out_specs=in_vmem,
        out_shape=shape_of(*rows.shape),
        compiler_params=params(6),
        cost_estimate=cost(0, 10 * rows.size),
    )(rows, weight, own, a, b)


def grad_kernel(rows_ref, above_ref, gain_ref, scale_ref, tilt_ref, own_ref, a_ref, b_ref, out_ref):
    width = rows_ref.shape[1]
    total = own_ref[...].astype(f32) + a_ref[...].astype(f32) + b_ref[...].astype(f32)
    rows = rows_ref[...].astype(f32)
    scale = scale_ref[:, :1].astype(bf16).astype(f32)
    cot = (total[:, :width] * scale + tilt_ref[...] * total[:, width : width + 1]) * gain_ref[...]
    inverse = lax.rsqrt(jnp.mean(rows * rows, axis=1, keepdims=True) + epsilon)
    along = jnp.mean(rows * cot, axis=1, keepdims=True) * (inverse * inverse * inverse)
    out_ref[...] = (above_ref[...].astype(f32) + (inverse * cot - rows * along)).astype(bf16)


def grad_call(rows, above, gain, scale, tilt, sums):
    return pl.pallas_call(
        grad_kernel,
        in_specs=[in_vmem] * (5 + len(sums)),
        out_specs=in_vmem,
        out_shape=shape_of(*rows.shape),
        compiler_params=params(16),
        cost_estimate=cost(0, 16 * rows.size),
    )(rows, above, gain, scale, tilt, *sums)


def place_kernel(select_ref, rows_ref, base_ref, out_ref):
    select = select_ref[...]
    one = jnp.ones((select.shape[0], 128), bf16)
    used = lax.dot_general(select, one, first_dims, preferred_element_type=f32)[:, :1] > 0
    for part in pieces_of(base_ref.shape[1], 6, 128):
        spread_rows = lax.dot_general(select, rows_ref[:, part], first_dims, preferred_element_type=f32)
        out_ref[:, part] = jnp.where(used, spread_rows.astype(bf16), base_ref[:, part])


def place_call(select, rows, base):
    return pl.pallas_call(
        place_kernel,
        in_specs=[in_vmem] * 3,
        out_specs=in_vmem,
        out_shape=shape_of(*base.shape),
        compiler_params=params(12),
        cost_estimate=cost(0, 4 * base.size),
    )(select, rows, base)


def route_kernel(after_ref, rows_ref, gain_ref, router_ref, ids_ref, weight_ref, *tilt_refs):
    ids, experts = ids_ref[...], router_ref.shape[0]
    select = select_of(ids).astype(bf16)
    rows = rows_ref[...].astype(f32)
    inverse = lax.rsqrt(jnp.mean(rows * rows, axis=1, keepdims=True) + epsilon)
    logits = lax.dot_general(
        rows * inverse * gain_ref[...], router_ref[...], last_dims, precision=highest, preferred_element_type=f32
    )
    expert = lax.broadcasted_iota(jnp.int32, (experts, ids.shape[1]), 0)
    first, second = (dot_t(select, (ids[k : k + 1] == expert).astype(bf16)) for k in (0, 1))
    share = jax.nn.sigmoid(jnp.sum((first - second) * logits, axis=1, keepdims=True))
    first_named, second_named = first[:, :1], second[:, :1]
    weight = share * first_named + (1.0 - share) * second_named
    weight_ref[...] = jnp.broadcast_to(weight, weight_ref.shape)
    for tilt_ref in tilt_refs:
        slant = share * (1.0 - share) * (first_named - second_named)
        tilt_ref[...] = jnp.dot(
            slant * (first - second), router_ref[...], precision=highest, preferred_element_type=f32
        )


def route_call(after, rows, gain, router_mat, ids, tilts):
    capacity, width = rows.shape
    return pl.pallas_call(
        route_kernel,
        in_specs=[anywhere] + [in_vmem] * 4,
        out_specs=[in_vmem] * (1 + tilts),
        out_shape=[shape_of(capacity, 128, f32)] + [shape_of(capacity, width, f32)] * tilts,
        compiler_params=params(20),
        cost_estimate=cost(0, 12 * rows.size),
    )(after, rows, gain, router_mat, ids)


def local(
    act_in, saved_in, grad_in, fwd_routes, bwd_routes, w_gate, w_up, w_down, router, norm_gain
):
    count = lax.axis_size("expert")
    gate, up, down = (pltpu.with_memory_space_constraint(array[0], pltpu.HBM) for array in (w_gate, w_up, w_down))
    router_mat = router[0].T
    fwd_ids, bwd_ids = fwd_routes[0].T, bwd_routes[0].T
    gather_f, gather_u, gather_h = Gather("f"), Gather("u"), Gather("h")
    scatter_o, scatter_r = Scatter("o"), Scatter("r")
    env = {"act_base": shifted(act_in[0], 1), "grad_base": shifted(grad_in[0], -1)}

    env["select_f"], env["rows_f"], normed_f = front_call(norm_gain, fwd_ids, act_in[0], norm_gain, 1)
    gather_f.begin(normed_f)

    def front_u(after):
        env["select_b"], rows = front_call(after, bwd_ids, grad_in[0], norm_gain, 0)
        env["rows_u"] = rows
        gather_u.begin(rows)
        return (rows[:16, :128],)

    def front_b(after):
        _, env["rows_b"], normed = front_call(after, bwd_ids, saved_in[0], norm_gain, 1)
        gather_h.begin(normed)
        return (normed[:16, :128],)

    def shifts(select_f):
        env["select_f_there"], env["select_b_there"] = shifted(select_f, 1), shifted(env["select_b"], -1)
        return ()

    def route_f(select_f):
        return tuple(route_call(select_f, env["rows_f"], norm_gain, router_mat, fwd_ids, 0))

    def route_b(select_f):
        return tuple(route_call(select_f, env["rows_b"], norm_gain, router_mat, bwd_ids, 1))

    def load(name, weight):
        def does(after):
            env[name], flag = load_call(after, weight)
            return (flag,)

        return does

    def active(after):
        return (active_call(gather_f.held, env["gate"], up),)

    def outpart(active):
        parts = outpart_call(count, active, env["down"])
        scatter_o.begin(parts)
        return (parts[0][0][:16, :128],)

    def back(after):
        return (back_call(gather_u.held, env["down"]),)

    def cots(back):
        return cots_call(gather_h.held, env["gate"], env["up"], back)

    def rowpart(gate_cot, up_cot, slope):
        parts = rowpart_call(count, gate_cot, up_cot, slope, env["gate"], env["up"])
        scatter_r.begin(parts)
        env["renewed"] = list(parts)
        return ()

    def act_rows(weight_f):
        rows = act_call(env["rows_f"], weight_f, scatter_o.parts[0][0], *scatter_o.inbox)
        env["act_rows"] = shifted(rows, 1)
        return ()

    def act_place(select, rows, base, other):
        return (place_call(select, rows, base),)

    last = gather_u.steps - 1
    turns = []
    for step in range(last):
        turns += [(gather_f, step), (gather_u, step) if step + 1 < last else (gather_h, 0)]
    turns += [(gather_f, last), (gather_u, last - 1), (gather_h, 1), (gather_u, last)]
    turns += [(gather_h, step) for step in range(2, last)]
    windows = [[turn] for turn in turns]
    windows += [[(scatter_o, 0)], [(gather_h, last), (scatter_o, 1)]]
    windows += [[(scatter_o, step)] for step in range(2, last + 1)]
    windows += [[(scatter_r, step)] for step in range(last + 1)]
    start = {turn: k for k, turns in enumerate(windows) for turn in turns}

    def stay(ring, step):
        return min(2, start.get((ring, step + 1), start[ring, step] + 2) - start[ring, step])

    windows = [[(ring, step, stay(ring, step)) for ring, step in turns] for turns in windows]
    windows[start[gather_h, last]] = [(gather_h, last, 1), (scatter_o, 1, 1)]
    windows[start[scatter_o, last]] = [(scatter_o, last, 1)]
    pieces = {}

    def put(window, needs, does, gives):
        pieces.setdefault(window, []).append((needs, does, gives))

    def nothing(*arrays):
        return ()

    f_done = start[gather_f, last] + 2
    h_done = start[gather_h, last] + 1
    out = start[scatter_o, last]
    put(0, ("select_f",), front_u, ("corner_u",))
    put(1, ("select_f",), front_b, ("corner_b",))
    put(2, ("select_f",), load("gate", gate), ("flag_g",))
    put(3, ("select_f",), load("down", down), ("flag_d",))
    put(f_done, ("select_f",), active, ("active",))
    put(f_done + 1, ("active",), outpart, ("corner_o",))
    put(h_done-3, ("act_base",), nothing, ())
    put(out+1, ("grad_base",), nothing, ())
    put(h_done - 2, ("select_f",), back, ("back",))
    put(h_done - 1, ("select_f",), load("up", up), ("flag_u",))
    put(h_done, ("back",), cots, ("gate_cot", "up_cot", "slope"))
    put(h_done + 1, ("gate_cot", "up_cot", "slope"), rowpart, ())
    put(out + 1, ("select_f",), shifts, ())
    put(out + 1, ("select_f",), route_f, ("weight_f",))
    put(out + 2, ("weight_f",), act_rows, ())
    put(out + 3, ("select_f",), route_b, ("scale", "tilt"))
    put(out + 4, ("select_f_there", "act_rows", "act_base", "select_b_there"), act_place, ("act_out",))
    run_windows(windows, pieces, env)

    sums = [scatter_r.parts[0][0], *scatter_r.inbox]
    grad_rows = grad_call(env["rows_b"], env["rows_u"], norm_gain, env["scale"], env["tilt"], sums)
    grad_out = place_call(env["select_b_there"], shifted(grad_rows, -1), env["grad_base"])
    return (env["act_out"][None], grad_out[None])


def solution(mesh):
    in_specs = (
        P("section", "expert", None),
        P("section", "expert", None),
        P("section", "expert", None),
        P("section", "expert", None),
        P("section", "expert", None),
        P("section", None, "expert"),
        P("section", None, "expert"),
        P("section", "expert", None),
        P("section", None, None),
        P("section", None),
    )
    out_specs = (P("section", "expert", None), P("section", "expert", None))
    return jax.shard_map(local, mesh=mesh, in_specs=in_specs, out_specs=out_specs, check_vma=False)
```

```python
import functools

import jax
import jax.numpy as jnp
from jax import lax
from jax.experimental import pallas as pl
from jax.experimental.pallas import tpu as pltpu
from jax.sharding import PartitionSpec as P

epsilon = 1e-05
highest = lax.Precision.HIGHEST
f32 = jnp.float32
bf16 = jnp.bfloat16
last_dims = (((1,), (1,)), ((), ()))
first_dims = (((0,), (0,)), ((), ()))
in_hbm = pl.BlockSpec(memory_space=pltpu.HBM)
anywhere = pl.BlockSpec(memory_space=pl.ANY)
in_vmem = pl.BlockSpec(memory_space=pltpu.VMEM)


def shape_of(rows, columns, dtype=bf16):
    return jax.ShapeDtypeStruct((rows, columns), dtype)


def params(mega):
    return pltpu.CompilerParams(vmem_limit_bytes=mega * 1024 * 1024)


def cost(flops, moved):
    return pl.CostEstimate(flops=int(flops), bytes_accessed=int(moved), transcendentals=0)


def dot_t(left, right):
    return lax.dot_general(left, right, last_dims, preferred_element_type=f32)


def dot_n(left, right):
    return jnp.dot(left, right, preferred_element_type=f32)


def hop(value, steps):
    count = lax.axis_size("expert")
    ring = list(range(0, count, 2)) + list(range(1, count, 2))[::-1]
    return lax.ppermute(value, "expert", [(ring[i], ring[(i + steps) % count]) for i in range(count)])


def shifted(value, steps):
    count = lax.axis_size("section")
    return lax.ppermute(value, "section", [(source, (source + steps) % count) for source in range(count)])


def halves(value):
    middle = value.shape[1] // 2
    return [value[:, :middle], value[:, middle:]]


class Ring:

    def __init__(self, name):
        self.name = name
        self.count = lax.axis_size("expert")
        self.full = (self.count - 1) // 2
        self.split = self.count % 2 == 0
        self.steps = self.full + self.split


class Gather(Ring):

    def begin(self, shard):
        self.held = [[shard]] + [None] * (self.count - 1)

    def send(self, step):
        ahead = self.held[-step % self.count][0]
        behind = self.held[step][0]
        if step == self.full:
            ahead, behind = halves(ahead)[0], halves(behind)[1]
        return [hop(ahead, 1), hop(behind, -1)]

    def receive(self, step, values):
        if step == self.full:
            self.held[step + 1] = values
        else:
            self.held[-1 - step], self.held[step + 1] = [values[0]], [values[1]]

    def sources(self, step):
        return [self.held[0]] if step == 0 else []


class Scatter(Ring):

    def begin(self, parts):
        self.parts = parts

    def send(self, step):
        far = self.steps - step
        if step > 0:
            ahead, behind = merge_call(self.parts[far][0], self.inbox[0], self.parts[-far][0], self.inbox[1])
        else:
            ahead, behind = self.parts[far][0], self.parts[-far][-1]
        return [hop(ahead, 1), hop(behind, -1)]

    def receive(self, step, values):
        self.inbox = values

    def sources(self, step):
        return [self.parts[self.steps]] + [self.parts[-self.steps]] * (1 - self.split) if step == 0 else []


def fence(arrays):
    return list(
        pl.pallas_call(
            lambda *refs: None,
            in_specs=[anywhere] * len(arrays),
            out_specs=[anywhere] * len(arrays),
            out_shape=[jax.ShapeDtypeStruct(array.shape, array.dtype) for array in arrays],
            compiler_params=params(1),
            cost_estimate=cost(0, 0),
            input_output_aliases={k: k for k in range(len(arrays))},
        )(*arrays)
    )


def run_windows(windows, pieces, env):
    flying, made = [], []
    for k, transfers in enumerate(windows):
        todo = pieces.get(k, [])
        names = list(made)
        for needs, _, _ in todo:
            names += [name for name in needs if name not in names]
        sources = env.pop("renewed", [])
        for ring, step, _ in transfers:
            sources += [held for held in ring.sources(step) if not any(held is other for other in sources)]
        landing = [flight for flight in flying if flight[2] <= k]
        flying = [flight for flight in flying if flight[2] > k]
        landed = [value for _, _, _, values in landing for value in values]
        passed = fence(landed + [env[name] for name in names] + [value for held in sources for value in held])
        for ring, step, _, values in landing:
            ring.receive(step, passed[: len(values)])
            passed = passed[len(values) :]
        for name in names:
            env[name] = passed.pop(0)
        for held in sources:
            held[:] = [passed.pop(0) for _ in held]
        with jax.named_scope(f"window_{k}"):
            flying += [(ring, step, k + stay, ring.send(step)) for ring, step, stay in transfers]
        made = []
        for needs, does, gives in todo:
            for name, value in zip(gives, does(*[env[name] for name in needs]), strict=True):
                env[name] = value
                made.append(name)
    for ring, step, _, values in flying:
        ring.receive(step, values)


def pieces_of(length, most, grain):
    for number in range(most, 1, -1):
        if length % (number * grain) == 0:
            size = length // number
            return [slice(k * size, (k + 1) * size) for k in range(number)]
    return [slice(0, length)]


def flat(held):
    return [value for shard in held for value in shard]


def row_copies(held_shape, shards, rows_ref, sems):
    side = rows_ref.shape[0] // len(held_shape)
    copies, at = [], 0
    for k, widths in enumerate(held_shape):
        first = 0
        for wide in widths:
            target = rows_ref.at[k * side : (k + 1) * side, first : first + wide]
            copies.append(pltpu.make_async_copy(shards[at], target, sems.at[at]))
            first, at = first + wide, at + 1
    return copies


def widths_of(held):
    return tuple(tuple(value.shape[1] for value in shard) for shard in held)


def start_all(*lists):
    for group in zip(*lists, strict=True):
        for copy in group:
            copy.start()


def merge_kernel(own_a_ref, value_a_ref, own_b_ref, value_b_ref, out_a_ref, out_b_ref):
    for own_ref, value_ref, out_ref, first in (
        (own_a_ref, value_a_ref, out_a_ref, 0),
        (own_b_ref, value_b_ref, out_b_ref, own_b_ref.shape[1] - value_b_ref.shape[1]),
    ):
        here = slice(first, first + value_ref.shape[1])
        if value_ref.shape != own_ref.shape:
            out_ref[...] = own_ref[...]
        out_ref[:, here] = (own_ref[:, here].astype(f32) + value_ref[...].astype(f32)).astype(bf16)


def merge_call(own_a, value_a, own_b, value_b):
    return pl.pallas_call(
        merge_kernel,
        in_specs=[in_vmem] * 4,
        out_specs=[in_vmem] * 2,
        out_shape=[shape_of(*own.shape) for own in (own_a, own_b)],
        compiler_params=params(4),
        cost_estimate=cost(0, 6 * own_a.size),
    )(own_a, value_a, own_b, value_b)


def load_kernel(after_ref, source, target, flag_ref, sems):
    copies = [
        pltpu.make_async_copy(source.at[part], target.at[part], sems.at[k])
        for k, part in enumerate(pieces_of(source.shape[0], 4, 128))
    ]
    start_all(copies)
    flag_ref[...] = jnp.zeros_like(flag_ref)
    for copy in copies:
        copy.wait()


def load_call(after, weight):
    return pl.pallas_call(
        load_kernel,
        in_specs=[anywhere, in_hbm],
        out_specs=[in_vmem, in_vmem],
        out_shape=[pltpu.VMEM(weight.shape, weight.dtype), shape_of(8, 128, f32)],
        scratch_shapes=[pltpu.SemaphoreType.DMA((4,))],
        compiler_params=params(1),
        cost_estimate=cost(0, 4 * weight.size),
    )(after, weight)


def back_kernel(held_shape, *refs):
    count = sum(len(widths) for widths in held_shape)
    shards, (down_ref, out_ref, rows_ref, row_sems) = refs[:count], refs[count:]
    parts = pieces_of(out_ref.shape[1], 4, 128)
    rows = row_copies(held_shape, shards, rows_ref, row_sems)
    start_all(rows)
    for copy in rows:
        copy.wait()
    for part in parts:
        out_ref[:, part] = dot_t(rows_ref[...], down_ref[part, :])


def back_call(held, down):
    count, side, width, hid = len(held), held[0][0].shape[0], sum(widths_of(held)[0]), down.shape[0]
    return pl.pallas_call(
        functools.partial(back_kernel, widths_of(held)),
        in_specs=[anywhere] * len(flat(held)) + [in_vmem],
        out_specs=in_vmem,
        out_shape=shape_of(count * side, hid, f32),
        scratch_shapes=[
            pltpu.VMEM((count * side, width), bf16),
            pltpu.SemaphoreType.DMA((len(flat(held)),)),
        ],
        compiler_params=params(8),
        cost_estimate=cost(2 * count * side * width * hid, 2 * width * (hid + count * side)),
    )(*flat(held), down)


def gate_up(held_shape, shards, gate_ref, up_ref, rows_ref, gate_sum, up_sum, up_w, row_sems, up_sems):
    parts = pieces_of(gate_ref.shape[0], 6, 128)
    rows = row_copies(held_shape, shards, rows_ref, row_sems)
    ups = [pltpu.make_async_copy(up_ref.at[part], up_w.at[part], up_sems.at[k]) for k, part in enumerate(parts)]
    start_all(rows)
    start_all(ups)
    for copy in rows:
        copy.wait()
    for k, part in enumerate(parts):
        product = dot_n(rows_ref[:, part], gate_ref[part, :])
        gate_sum[...] = product if k == 0 else gate_sum[...] + product
    for k, part in enumerate(parts):
        ups[k].wait()
        product = dot_n(rows_ref[:, part], up_w[part, :])
        up_sum[...] = product if k == 0 else up_sum[...] + product


def gate_up_held(held_shape, shards, gate_ref, up_ref, rows_ref, gate_sum, up_sum, row_sems):
    rows = row_copies(held_shape, shards, rows_ref, row_sems)
    start_all(rows)
    for copy in rows:
        copy.wait()
    for k, part in enumerate(pieces_of(gate_ref.shape[0], 6, 128)):
        for weight, total in ((gate_ref, gate_sum), (up_ref, up_sum)):
            product = dot_n(rows_ref[:, part], weight[part, :])
            total[...] = product if k == 0 else total[...] + product


def gate_up_scratch(copies, count, side, width, hid, held=False):
    sums = [pltpu.VMEM((count * side, hid), f32)] * 2
    loads = [] if held else [pltpu.VMEM((width, hid), bf16)]
    sems = [pltpu.SemaphoreType.DMA((copies,))] + [pltpu.SemaphoreType.DMA((6,))] * (not held)
    return [pltpu.VMEM((count * side, width), bf16), *sums, *loads, *sems]


def gate_up_cost(count, side, width, hid):
    return cost(4 * count * side * width * hid, 2 * width * (2 * hid + count * side))


def active_kernel(held_shape, *refs):
    count = sum(len(widths) for widths in held_shape)
    shards, (gate_ref, up_ref, out_ref, *scratch) = refs[:count], refs[count:]
    gate_up(held_shape, shards, gate_ref, up_ref, *scratch)
    gate_pre = scratch[1][...]
    out_ref[...] = (gate_pre * jax.nn.sigmoid(gate_pre) * scratch[2][...]).astype(bf16)


def active_call(held, gate, up):
    count, side, width, hid = len(held), held[0][0].shape[0], sum(widths_of(held)[0]), gate.shape[1]
    return pl.pallas_call(
        functools.partial(active_kernel, widths_of(held)),
        in_specs=[anywhere] * len(flat(held)) + [in_vmem, in_hbm],
        out_specs=in_vmem,
        out_shape=shape_of(count * side, hid),
        scratch_shapes=gate_up_scratch(len(flat(held)), count, side, width, hid),
        compiler_params=params(24),
        cost_estimate=gate_up_cost(count, side, width, hid),
    )(*flat(held), gate, up)


def cots_kernel(held_shape, *refs):
    count = sum(len(widths) for widths in held_shape)
    shards, (gate_ref, up_ref, back_ref, gate_cot_ref, up_cot_ref, slope_ref, *scratch) = refs[:count], refs[count:]
    gate_up_held(held_shape, shards, gate_ref, up_ref, *scratch)
    gate_pre, up_pre = scratch[1][...], scratch[2][...]
    sig = jax.nn.sigmoid(gate_pre)
    silu = gate_pre * sig
    back = back_ref[...]
    active = (silu * up_pre).astype(bf16).astype(f32)
    slope_ref[...] = jnp.broadcast_to(jnp.sum(active * back, axis=1, keepdims=True), slope_ref.shape)
    gate_cot_ref[...] = (back * up_pre * sig * (1.0 + gate_pre * (1.0 - sig))).astype(bf16)
    up_cot_ref[...] = (back * silu).astype(bf16)


def cots_call(held, gate, up, back):
    count, side, width, hid = len(held), held[0][0].shape[0], sum(widths_of(held)[0]), gate.shape[1]
    return pl.pallas_call(
        functools.partial(cots_kernel, widths_of(held)),
        in_specs=[anywhere] * len(flat(held)) + [in_vmem] * 3,
        out_specs=[in_vmem] * 3,
        out_shape=[
            shape_of(count * side, hid),
            shape_of(count * side, hid),
            shape_of(count * side, 128, f32),
        ],
        scratch_shapes=gate_up_scratch(len(flat(held)), count, side, width, hid, True),
        compiler_params=params(14),
        cost_estimate=gate_up_cost(count, side, width, hid),
    )(*flat(held), gate, up, back)


def segments(count, width, extra):
    whole, pair = [(0, width + extra)], [(0, width // 2), (width // 2, width + extra)]
    return [pair if 2 * k == count else whole for k in range(count)]


def part_shapes(side, held):
    return [shape_of(side, last - first) for ranges in held for first, last in ranges]


def spread(made, held, first, value):
    side, last, at = value.shape[0] // len(held), first + value.shape[1], 0
    for k, ranges in enumerate(held):
        for low, high in ranges:
            begin, end = max(first, low), min(last, high)
            if begin < end:
                rows = value[k * side : (k + 1) * side, begin - first : end - first]
                made[at][:, begin - low : end - low] = rows
            at += 1


def send_out(made, out_refs, sems):
    copies = [
        pltpu.make_async_copy(source, target, sems.at[at])
        for at, (source, target) in enumerate(zip(made, out_refs, strict=True))
    ]
    start_all(copies)
    for copy in copies:
        copy.wait()


def made_scratch(shapes):
    return [pltpu.VMEM(shape.shape, shape.dtype) for shape in shapes] + [pltpu.SemaphoreType.DMA((len(shapes),))]


def regroup(held, arrays):
    arrays = list(arrays)
    return [[arrays.pop(0) for _ in ranges] for ranges in held]


def outpart_kernel(held, active_ref, down_ref, *refs):
    number = sum(len(ranges) for ranges in held)
    out_refs, made, (out_sems,) = refs[:number], refs[number : 2 * number], refs[2 * number :]
    width = down_ref.shape[1]
    parts = pieces_of(width, 6, 128)
    for part in parts:
        value = dot_n(active_ref[...], down_ref[:, part])
        spread(made, held, part.start, value.astype(bf16))
    send_out(made, out_refs, out_sems)


def outpart_call(count, active, down):
    rows, (hid, width) = active.shape[0], down.shape
    held = segments(count, width, 0)
    shapes = part_shapes(rows // count, held)
    arrays = pl.pallas_call(
        functools.partial(outpart_kernel, held),
        in_specs=[in_vmem] * 2,
        out_specs=[anywhere] * len(shapes),
        out_shape=shapes,
        scratch_shapes=made_scratch(shapes),
        compiler_params=params(6),
        cost_estimate=cost(2 * rows * width * hid, 2 * width * hid),
    )(active, down)
    return regroup(held, arrays)


def rowpart_kernel(held, gate_cot_ref, up_cot_ref, slope_ref, gate_ref, up_ref, *out_refs):
    width = gate_ref.shape[0]
    parts = pieces_of(width, 6, 128)

    spread(out_refs, held, width, slope_ref[...].astype(bf16))
    for part in parts:
        value = dot_t(gate_cot_ref[...], gate_ref[part, :]) + dot_t(up_cot_ref[...], up_ref[part, :])
        spread(out_refs, held, part.start, value.astype(bf16))


def rowpart_call(count, gate_cot, up_cot, slope, gate, up):
    rows, (width, hid) = gate_cot.shape[0], gate.shape
    held = segments(count, width, slope.shape[1])
    shapes = part_shapes(rows // count, held)
    arrays = pl.pallas_call(
        functools.partial(rowpart_kernel, held),
        in_specs=[in_vmem] * 5,
        out_specs=[in_vmem] * len(shapes),
        out_shape=shapes,
        compiler_params=params(6),
        cost_estimate=cost(4 * rows * width * hid, 4 * width * hid),
    )(gate_cot, up_cot, slope, gate, up)
    return regroup(held, arrays)


def select_of(ids):
    tokens = ids.shape[1]
    capacity = tokens // 4
    named = jnp.max((ids == 0).astype(f32), axis=0, keepdims=True)
    row = lax.broadcasted_iota(jnp.int32, (tokens, tokens), 0)
    column = lax.broadcasted_iota(jnp.int32, (tokens, tokens), 1)
    earlier = (row < column).astype(bf16)
    rank = dot_n(jnp.broadcast_to(named, (8, tokens)).astype(bf16), earlier)[:1]
    slot = jnp.where(named > 0, rank, float(capacity))
    places = lax.broadcasted_iota(jnp.int32, (capacity, tokens), 0).astype(f32)
    return (slot == places).astype(f32)


def pick(select, values):
    return dot_n(select.astype(bf16), values)


def front_kernel(after_ref, ids_hbm, values_hbm, gain_hbm, *refs):
    select_ref, rows_ref, *normed_refs = refs[:-4]
    ids_ref, values_ref, gain_ref, sems = refs[-4:]
    copies = [
        pltpu.make_async_copy(source, target, sems.at[k])
        for k, (source, target) in enumerate(
            ((ids_hbm, ids_ref), (values_hbm, values_ref), (gain_hbm, gain_ref))
        )
    ]
    start_all(copies)
    copies[0].wait()
    select = select_of(ids_ref[...])
    select_ref[...] = select.astype(bf16)
    copies[1].wait()
    rows = pick(select, values_ref[...])
    rows_ref[...] = rows.astype(bf16)
    copies[2].wait()
    for normed_ref in normed_refs:
        inverse = lax.rsqrt(jnp.mean(rows * rows, axis=1, keepdims=True) + epsilon)
        normed_ref[...] = (rows * inverse * gain_ref[...]).astype(bf16)


def front_call(after, ids, values, gain, normed):
    tokens, width = values.shape
    capacity = tokens // 4
    ids, values, gain = (pltpu.with_memory_space_constraint(array, pltpu.HBM) for array in (ids, values, gain))
    return pl.pallas_call(
        front_kernel,
        in_specs=[anywhere] + [in_hbm] * 3,
        out_specs=[in_vmem] * (2 + normed),
        out_shape=[shape_of(capacity, tokens)] + [shape_of(capacity, width)] * (1 + normed),
        scratch_shapes=[
            pltpu.VMEM(ids.shape, ids.dtype),
            pltpu.VMEM(values.shape, values.dtype),
            pltpu.VMEM(gain.shape, gain.dtype),
            pltpu.SemaphoreType.DMA((3,)),
        ],
        compiler_params=params(8),
        cost_estimate=cost(0, 8 * values.size),
    )(after, ids, values, gain)


def act_kernel(rows_ref, weight_ref, own_ref, a_ref, b_ref, out_ref):
    total = own_ref[...].astype(f32) + a_ref[...].astype(f32) + b_ref[...].astype(f32)
    out_ref[...] = (rows_ref[...].astype(f32) + weight_ref[:, :1] * total).astype(bf16)


def act_call(rows, weight, own, a, b):
    return pl.pallas_call(
        act_kernel,
        in_specs=[in_vmem] * 5,
        out_specs=in_vmem,
        out_shape=shape_of(*rows.shape),
        compiler_params=params(6),
        cost_estimate=cost(0, 10 * rows.size),
    )(rows, weight, own, a, b)


def grad_kernel(rows_ref, above_ref, gain_ref, scale_ref, tilt_ref, own_ref, a_ref, b_ref, out_ref):
    width = rows_ref.shape[1]
    total = own_ref[...].astype(f32) + a_ref[...].astype(f32) + b_ref[...].astype(f32)
    rows = rows_ref[...].astype(f32)
    scale = scale_ref[:, :1].astype(bf16).astype(f32)
    cot = (total[:, :width] * scale + tilt_ref[...] * total[:, width : width + 1]) * gain_ref[...]
    inverse = lax.rsqrt(jnp.mean(rows * rows, axis=1, keepdims=True) + epsilon)
    along = jnp.mean(rows * cot, axis=1, keepdims=True) * (inverse * inverse * inverse)
    out_ref[...] = (above_ref[...].astype(f32) + (inverse * cot - rows * along)).astype(bf16)


def grad_call(rows, above, gain, scale, tilt, sums):
    return pl.pallas_call(
        grad_kernel,
        in_specs=[in_vmem] * (5 + len(sums)),
        out_specs=in_vmem,
        out_shape=shape_of(*rows.shape),
        compiler_params=params(16),
        cost_estimate=cost(0, 16 * rows.size),
    )(rows, above, gain, scale, tilt, *sums)


def place_kernel(select_ref, rows_ref, base_ref, out_ref, made, sems):
    select = select_ref[...]
    one = jnp.ones((select.shape[0], 128), bf16)
    used = lax.dot_general(select, one, first_dims, preferred_element_type=f32)[:, :1] > 0
    copies = []
    for k, part in enumerate(pieces_of(base_ref.shape[1], 6, 128)):
        spread_rows = lax.dot_general(select, rows_ref[:, part], first_dims, preferred_element_type=f32)
        made[:, part] = jnp.where(used, spread_rows.astype(bf16), base_ref[:, part])
        copies.append(pltpu.make_async_copy(made.at[:, part], out_ref.at[:, part], sems.at[k]))
        copies[-1].start()
    for copy in copies:
        copy.wait()


def place_call(select, rows, base):
    return pl.pallas_call(
        place_kernel,
        in_specs=[in_vmem] * 3,
        out_specs=anywhere,
        out_shape=shape_of(*base.shape),
        scratch_shapes=[pltpu.VMEM(base.shape, bf16), pltpu.SemaphoreType.DMA((6,))],
        compiler_params=params(12),
        cost_estimate=cost(0, 4 * base.size),
    )(select, rows, base)


def route_kernel(after_ref, rows_ref, gain_ref, router_ref, ids_ref, weight_ref, *tilt_refs):
    ids, experts = ids_ref[...], router_ref.shape[0]
    select = select_of(ids).astype(bf16)
    rows = rows_ref[...].astype(f32)
    inverse = lax.rsqrt(jnp.mean(rows * rows, axis=1, keepdims=True) + epsilon)
    logits = lax.dot_general(
        rows * inverse * gain_ref[...], router_ref[...], last_dims, precision=highest, preferred_element_type=f32
    )
    expert = lax.broadcasted_iota(jnp.int32, (experts, ids.shape[1]), 0)
    first, second = (dot_t(select, (ids[k : k + 1] == expert).astype(bf16)) for k in (0, 1))
    share = jax.nn.sigmoid(jnp.sum((first - second) * logits, axis=1, keepdims=True))
    first_named, second_named = first[:, :1], second[:, :1]
    weight = share * first_named + (1.0 - share) * second_named
    weight_ref[...] = jnp.broadcast_to(weight, weight_ref.shape)
    for tilt_ref in tilt_refs:
        slant = share * (1.0 - share) * (first_named - second_named)
        tilt_ref[...] = jnp.dot(
            slant * (first - second), router_ref[...], precision=highest, preferred_element_type=f32
        )


def route_call(after, rows, gain, router_mat, ids, tilts):
    capacity, width = rows.shape
    return pl.pallas_call(
        route_kernel,
        in_specs=[anywhere] + [in_vmem] * 4,
        out_specs=[in_vmem] * (1 + tilts),
        out_shape=[shape_of(capacity, 128, f32)] + [shape_of(capacity, width, f32)] * tilts,
        compiler_params=params(20),
        cost_estimate=cost(0, 12 * rows.size),
    )(after, rows, gain, router_mat, ids)


def local(
    act_in, saved_in, grad_in, fwd_routes, bwd_routes, w_gate, w_up, w_down, router, norm_gain
):
    count = lax.axis_size("expert")
    gate, up, down = (pltpu.with_memory_space_constraint(array[0], pltpu.HBM) for array in (w_gate, w_up, w_down))
    router_mat = router[0].T
    fwd_ids, bwd_ids = fwd_routes[0].T, bwd_routes[0].T
    gather_f, gather_u, gather_h = Gather("f"), Gather("u"), Gather("h")
    scatter_o, scatter_r = Scatter("o"), Scatter("r")
    env = {"act_base": shifted(act_in[0], 1), "grad_base": shifted(grad_in[0], -1)}

    env["select_f"], env["rows_f"], normed_f = front_call(norm_gain, fwd_ids, act_in[0], norm_gain, 1)
    gather_f.begin(normed_f)

    def front_u(after):
        env["select_b"], rows = front_call(after, bwd_ids, grad_in[0], norm_gain, 0)
        env["rows_u"] = rows
        gather_u.begin(rows)
        return (rows[:16, :128],)

    def front_b(after):
        _, env["rows_b"], normed = front_call(after, bwd_ids, saved_in[0], norm_gain, 1)
        gather_h.begin(normed)
        return (normed[:16, :128],)

    def shifts(select_f):
        env["select_f_there"], env["select_b_there"] = shifted(select_f, 1), shifted(env["select_b"], -1)
        return ()

    def route_f(select_f):
        return tuple(route_call(select_f, env["rows_f"], norm_gain, router_mat, fwd_ids, 0))

    def route_b(select_f):
        return tuple(route_call(select_f, env["rows_b"], norm_gain, router_mat, bwd_ids, 1))

    def load(name, weight):
        def does(after):
            env[name], flag = load_call(after, weight)
            return (flag,)

        return does

    def active(after):
        return (active_call(gather_f.held, env["gate"], up),)

    def outpart(active):
        parts = outpart_call(count, active, env["down"])
        scatter_o.begin(parts)
        return (parts[0][0][:16, :128],)

    def back(after):
        return (back_call(gather_u.held, env["down"]),)

    def cots(back):
        return cots_call(gather_h.held, env["gate"], env["up"], back)

    def rowpart(gate_cot, up_cot, slope):
        parts = rowpart_call(count, gate_cot, up_cot, slope, env["gate"], env["up"])
        scatter_r.begin(parts)
        env["renewed"] = list(parts)
        return ()

    def act_rows(weight_f):
        rows = act_call(env["rows_f"], weight_f, scatter_o.parts[0][0], *scatter_o.inbox)
        env["act_rows"] = shifted(rows, 1)
        return ()

    def act_place(select, rows, base, other):
        return (place_call(select, rows, base),)

    last = gather_u.steps - 1
    turns = []
    for step in range(last):
        turns += [(gather_f, step), (gather_u, step) if step + 1 < last else (gather_h, 0)]
    turns += [(gather_f, last), (gather_u, last - 1), (gather_h, 1), (gather_u, last)]
    turns += [(gather_h, step) for step in range(2, last)]
    windows = [[turn] for turn in turns]
    windows += [[(scatter_o, 0)], [(gather_h, last), (scatter_o, 1)]]
    windows += [[(scatter_o, step)] for step in range(2, last + 1)]
    windows += [[(scatter_r, step)] for step in range(last + 1)]
    start = {turn: k for k, turns in enumerate(windows) for turn in turns}

    def stay(ring, step):
        return min(2, start.get((ring, step + 1), start[ring, step] + 2) - start[ring, step])

    windows = [[(ring, step, stay(ring, step)) for ring, step in turns] for turns in windows]
    windows[start[gather_h, last]] = [(gather_h, last, 1), (scatter_o, 1, 1)]
    windows[start[scatter_o, last]] = [(scatter_o, last, 1)]
    pieces = {}

    def put(window, needs, does, gives):
        pieces.setdefault(window, []).append((needs, does, gives))

    def nothing(*arrays):
        return ()

    f_done = start[gather_f, last] + 2
    h_done = start[gather_h, last] + 1
    out = start[scatter_o, last]
    put(0, ("select_f",), front_u, ("corner_u",))
    put(1, ("select_f",), front_b, ("corner_b",))
    put(2, ("select_f",), load("gate", gate), ("flag_g",))
    put(3, ("select_f",), load("down", down), ("flag_d",))
    put(f_done, ("select_f",), active, ("active",))
    put(f_done + 1, ("active",), outpart, ("corner_o",))
    put(h_done - 3, ("act_base",), nothing, ())
    put(out + 2, ("grad_base",), nothing, ())
    put(h_done - 2, ("select_f",), back, ("back",))
    put(h_done - 1, ("select_f",), load("up", up), ("flag_u",))
    put(h_done, ("back",), cots, ("gate_cot", "up_cot", "slope"))
    put(h_done + 1, ("gate_cot", "up_cot", "slope"), rowpart, ())
    put(out + 1, ("select_f",), shifts, ())
    put(out + 1, ("select_f",), route_f, ("weight_f",))
    put(out + 2, ("weight_f",), act_rows, ())
    put(out + 3, ("select_f",), route_b, ("scale", "tilt"))
    put(out + 4, ("select_f_there", "act_rows", "act_base", "select_b_there"), act_place, ("act_out",))
    run_windows(windows, pieces, env)

    sums = [scatter_r.parts[0][0], *scatter_r.inbox]
    grad_rows = grad_call(env["rows_b"], env["rows_u"], norm_gain, env["scale"], env["tilt"], sums)
    grad_out = place_call(env["select_b_there"], shifted(grad_rows, -1), env["grad_base"])
    return (env["act_out"][None], grad_out[None])


def solution(mesh):
    in_specs = (
        P("section", "expert", None),
        P("section", "expert", None),
        P("section", "expert", None),
        P("section", "expert", None),
        P("section", "expert", None),
        P("section", None, "expert"),
        P("section", None, "expert"),
        P("section", "expert", None),
        P("section", None, None),
        P("section", None),
    )
    out_specs = (P("section", "expert", None), P("section", "expert", None))
    return jax.shard_map(local, mesh=mesh, in_specs=in_specs, out_specs=out_specs, check_vma=False)
```
